128 devices in a mesh: az: 16 (over y, x_lo, core), rad: 8 (over x_hi, z).
Axes of the slice: x: 4 (x_hi: 2, x_lo: 2; x = x_hi * 2 + x_lo), y: 4, z: 4, core: 2. Of those that a mesh axis runs over, the one named last changes fastest.
Arguments:
- density: float32 [128, 64, 4096], P('rad', None, 'az'), may hold values from 0.5 to 2
- momenta: float32 [3, 128, 64, 4096], P(None, 'rad', None, 'az'), may hold values from -0.75 to 0.75
- energy: float32 [128, 64, 4096], P('rad', None, 'az'), may hold values from 0.5 to 2
- shifts: int32 [128], P('rad'), may hold values from 0 to 4095, as said below
Outputs:
- density_next: float32 [128, 64, 4096], P('rad', None, 'az')
- momenta_next: float32 [3, 128, 64, 4096], P(None, 'rad', None, 'az')
- energy_next: float32 [128, 64, 4096], P('rad', None, 'az')
The draws below stay inside these ranges and needn't reach their ends.
Inputs may be any that keep to these rules, and one draw needn't show every extreme that they name: `shifts`: any shift of 0 to 4095 may occur; both ends occur.
All inputs are finite; a program needn't handle non-finite values.
Results may differ from the reference program's by a relative error of at most 0.0003.
Values sent between devices are 32-bit elements; how exact they have to be, the bound alone decides.
A program may use at most 192 MiB of HBM per device.

```python
import math
import jax
import jax.numpy as jnp

NTH = 64
NR = 128
NPHI = 4096


def draw_shifts(key, part):
    key = jax.random.fold_in(key, 7)
    keys = jax.random.split(key, 3)
    values = jax.random.randint(keys[0], (NR,), 0, NPHI, dtype=jnp.int32)
    half = NR // 2
    first = jax.random.randint(keys[1], (), 0, half, dtype=jnp.int32)
    second = half + jax.random.randint(keys[2], (), 0, NR - half, dtype=jnp.int32)
    values = values.at[first].set(NPHI - 1)
    values = values.at[second].set(0)
    return values


def block_scale(key, extent, cuts, smallest, high):
    def one(dim, shards_of):
        heights = jax.random.uniform(jax.random.fold_in(jax.random.fold_in(key, 6), dim), (shards_of,), jnp.float32, smallest / len(cuts), high / len(cuts))
        return jnp.repeat(jnp.exp(heights), extent[dim] // shards_of).reshape((-1,) + (1,) * (len(extent) - dim - 1))

    factor_of = one(*cuts[0])
    for cut in cuts[1:]:
        factor_of = factor_of * one(*cut)
    return factor_of


def normal_values(rng, shape, width, limit, cuts=(), kind=jnp.bfloat16):
    values = width * jax.random.normal(rng, shape, jnp.float32)
    if cuts:
        values = values * block_scale(rng, shape, cuts, -0.22, 0.18)
    return jnp.clip(values, -limit, limit).astype(kind)


def setup_inputs(seed: int = 0) -> dict:
    seeds = jax.random.split(jax.random.key(seed), 5)
    return {
        "density": jnp.clip(jnp.exp(math.log(2.0) - 1.3862944 * jax.random.uniform(seeds[0], (NR, NTH, NPHI), jnp.float32) ** block_scale(seeds[0], (NR, NTH, NPHI), ((0, 8), (2, 16)), -0.2, 0.2)), 0.5, 2.0),
        "momenta": normal_values(seeds[1], (3, NR, NTH, NPHI), 0.05, 0.75, ((1, 8), (3, 16)), jnp.float32),
        "energy": jnp.clip(jnp.exp(math.log(2.0) - 1.3862944 * jax.random.uniform(seeds[2], (NR, NTH, NPHI), jnp.float32) ** block_scale(seeds[2], (NR, NTH, NPHI), ((0, 8), (2, 16)), -0.2, 0.2)), 0.5, 2.0),
        "shifts": draw_shifts(jax.random.fold_in(seeds[4], 71), 0),
    }


def advance(padded, at_inner, at_outer, radius):
    rows = padded.shape[1] - 2
    rho = padded[0]
    vel_r = padded[1] / rho
    core = padded[:, :, :, 1:-1]
    face_r = 0.5 * (vel_r[:-1] + vel_r[1:])[:, :, 1:-1]
    flux_r = face_r * jnp.where(face_r > 0, core[:, :-1], core[:, 1:])
    faces = jnp.arange(rows + 1)
    keep = jnp.where((faces == 0) & at_inner, 0.0, 1.0)
    keep = jnp.where((faces == rows) & at_outer, 0.0, keep).astype(jnp.float32)
    flux_r = flux_r * keep[None, :, None, None]
    face_rad = 0.5 * (radius[:-1] + radius[1:])
    centre = radius[1:-1]
    weighted = flux_r * (face_rad * face_rad)[None, :, None, None]
    div_r = (weighted[:, 1:] - weighted[:, :-1]) / (centre * centre)[None, :, None, None]
    inner = padded[:, 1:-1]
    rho_in = inner[0]
    vel_p = inner[2] / rho_in
    vel_t = inner[3] / rho_in
    qcore = inner[..., 1:-1]
    vt_core = vel_t[..., 1:-1]
    face_t = 0.5 * (vt_core[:, :-1] + vt_core[:, 1:])
    flux_t = face_t * jnp.where(face_t > 0, qcore[:, :, :-1], qcore[:, :, 1:])
    zero_t = jnp.zeros_like(flux_t[:, :, :1])
    flux_t = jnp.concatenate([zero_t, flux_t, zero_t], axis=2)
    div_t = flux_t[:, :, 1:] - flux_t[:, :, :-1]
    face_p = 0.5 * (vel_p[..., :-1] + vel_p[..., 1:])
    flux_p = face_p * jnp.where(face_p > 0, inner[..., :-1], inner[..., 1:])
    div_p = flux_p[..., 1:] - flux_p[..., :-1]
    moved = qcore - div_r - div_t - div_p
    pressure = 0.4 * padded[4]
    grad_r = 0.5 * (pressure[2:, :, 1:-1] - pressure[:-2, :, 1:-1])
    grad_p = 0.5 * (pressure[1:-1, :, 2:] - pressure[1:-1, :, :-2])
    middle = pressure[1:-1, :, 1:-1]
    edged = jnp.concatenate([middle[:, :1], middle, middle[:, -1:]], axis=1)
    grad_t = 0.5 * (edged[:, 2:] - edged[:, :-2])
    pushed = moved[1:4] - 0.5 * jnp.stack([grad_r, grad_p, grad_t])
    return jnp.concatenate([moved[:1], pushed, moved[4:]], axis=0)


def reference(density, momenta, energy, shifts):
    state = jnp.concatenate([density[None], momenta, energy[None]], axis=0)
    padded = jnp.pad(state, ((0, 0), (1, 1), (0, 0), (0, 0)), mode="edge")
    padded = jnp.concatenate([padded[..., -1:], padded, padded[..., :1]], axis=3)
    index = jnp.arange(-1, NR + 1).astype(jnp.float32)
    radius = 1.0 + 2.0 * (index + 0.5) / NR
    sourced = advance(padded, True, True, radius)
    cells = jnp.arange(NPHI, dtype=jnp.int32)

    def loop(row, amount):
        source = jnp.mod(cells - amount, NPHI).astype(jnp.int32)
        return jnp.take(row, source, axis=-1)

    out = jax.vmap(loop, in_axes=(1, 0), out_axes=1)(sourced, shifts)
    return out[0], out[1:4], out[4]
```

```python
import functools

import jax
import jax.numpy as jnp
from jax import lax
from jax.experimental import pallas as pl
from jax.experimental.pallas import tpu as pltpu
from jax.sharding import PartitionSpec as P

MESH = pl.DeviceIdType.MESH
LANES = 128
SUB = 8
FIELDS = 5


def remote(src, dst, send, recv, **where):
    return pltpu.make_async_remote_copy(
        src_ref=src, dst_ref=dst, send_sem=send, recv_sem=recv, device_id=where, device_id_type=MESH
    )


def wait_bytes(ref, sem):
    pltpu.make_async_copy(ref, ref, sem).wait()


def peer(me, k):
    y = (me // 4 + k // 4) % 4
    x = (me // 2 + k // 2) % 2
    core = (me + k) % 2
    return y * 4 + x * 2 + core


def kernel(chunks, early, den, mom, en, shifts, landed, *refs):
    amounts, st, send, turned, pack, halo = refs[:6]
    whole = refs[6 : 6 + chunks]
    in_sem, rad_send, rad_recv, az_send, az_recv, s1, r1, own1, s2, r2, own2 = refs[6 + chunks :]
    rows = den.shape[0]
    tiles = den.shape[1] // SUB
    per = tiles // chunks
    me = lax.axis_index("az")
    n = lax.axis_size("az")
    pos = lax.axis_index("rad")
    groups = lax.axis_size("rad")
    at_inner = pos == 0
    at_outer = pos == groups - 1

    loads = [
        pltpu.make_async_copy(den, st.at[0, pl.ds(1, rows)], in_sem.at[0]),
        pltpu.make_async_copy(mom, st.at[pl.ds(1, 3), pl.ds(1, rows)], in_sem.at[1]),
        pltpu.make_async_copy(en, st.at[4, pl.ds(1, rows)], in_sem.at[2]),
        pltpu.make_async_copy(shifts, amounts, in_sem.at[3]),
    ]
    for c in loads:
        c.start()

    barrier = pltpu.get_barrier_semaphore()

    def greet(k, _):
        pl.semaphore_signal(barrier, 1, device_id={"az": peer(me, k)}, device_id_type=MESH)
        return 0

    lax.fori_loop(1, n, greet, 0)

    @pl.when(jnp.logical_not(at_outer))
    def _():
        pl.semaphore_signal(barrier, 1, device_id={"rad": pos + 1}, device_id_type=MESH)

    @pl.when(jnp.logical_not(at_inner))
    def _():
        pl.semaphore_signal(barrier, 1, device_id={"rad": pos - 1}, device_id_type=MESH)

    apart = jnp.where(at_inner, 0, 1) + jnp.where(at_outer, 0, 1)
    pl.semaphore_wait(barrier, n - 1 + apart)

    def radial(row, slot, way, to):
        return [
            remote(den.at[row], st.at[0, slot], rad_send.at[way, 0], rad_recv.at[way, 0], rad=to),
            remote(mom.at[:, row], st.at[pl.ds(1, 3), slot], rad_send.at[way, 1], rad_recv.at[way, 1], rad=to),
            remote(en.at[row], st.at[4, slot], rad_send.at[way, 2], rad_recv.at[way, 2], rad=to),
        ]

    outward = radial(rows - 1, 0, 0, (pos + 1) % groups)
    inward = radial(0, rows + 1, 1, (pos + groups - 1) % groups)

    @pl.when(jnp.logical_not(at_outer))
    def _():
        for c in outward:
            c.start()

    @pl.when(jnp.logical_not(at_inner))
    def _():
        for c in inward:
            c.start()

    for c in loads:
        c.wait()

    lane = lax.broadcasted_iota(jnp.int32, (SUB, LANES), 1)
    sub = lax.broadcasted_iota(jnp.int32, (SUB, LANES), 0)

    def packing(t, _):
        at = pl.ds(pl.multiple_of(t * SUB, SUB), SUB)
        first = jnp.zeros((SUB, LANES), jnp.float32)
        last = jnp.zeros((SUB, LANES), jnp.float32)
        for f in range(FIELDS):
            for i in range(rows):
                k = f * rows + i
                low = st[f, 1 + i, at, 0:LANES]
                high = st[f, 1 + i, at, LANES : 2 * LANES]
                first = jnp.where(lane == k, pltpu.roll(low, k, 1) if k else low, first)
                last = jnp.where(lane == k, pltpu.roll(high, k + 1, 1), last)
        pack[0, t] = first
        pack[1, t] = last
        return 0

    lax.fori_loop(0, tiles, packing, 0)
    right = remote(pack.at[1], halo.at[0], az_send.at[0], az_recv.at[0], az=(me + 1) % n)
    left = remote(pack.at[0], halo.at[1], az_send.at[1], az_recv.at[1], az=(me + n - 1) % n)
    right.start()
    left.start()

    total = (groups * rows)

    def radius(index):
        return 1.0 + 2.0 * (index.astype(jnp.float32) + 0.5) / total

    def upwind(face, low, high):
        return face * jnp.where(face > 0, low, high)

    def compute(row, t):
        t0 = pl.multiple_of(t * SUB, SUB)
        at = pl.ds(t0, SUB)
        at_dn = pl.ds(pl.multiple_of(jnp.maximum(t - 1, 0) * SUB, SUB), SUB)
        at_up = pl.ds(pl.multiple_of(jnp.minimum(t + 1, tiles - 1) * SUB, SUB), SUB)
        index = pos * rows + row
        here = radius(index)
        face_up = 0.5 * (here + radius(index + 1))
        face_dn = 0.5 * (radius(index - 1) + here)
        area = jnp.full((SUB, LANES), here * here, jnp.float32)
        w_up = jnp.full((SUB, LANES), face_up * face_up, jnp.float32) / area
        w_dn = jnp.full((SUB, LANES), face_dn * face_dn, jnp.float32) / area
        w_up = jnp.where(index == total - 1, 0.0, w_up)
        w_dn = jnp.where(index == 0, 0.0, w_dn)
        before = halo[0, t]
        after = halo[1, t]
        q = [[st[f, row + 1, at, h * LANES : (h + 1) * LANES] for h in range(2)] for f in range(FIELDS)]
        back, ahead = [], []
        for f in range(FIELDS):
            k = f * rows + row
            b = pltpu.roll(before, (LANES - k) % LANES, 1)
            a = pltpu.roll(after, LANES - 1 - k, 1)
            low, high = q[f]
            low_r, high_r = pltpu.roll(low, 1, 1), pltpu.roll(high, 1, 1)
            low_l, high_l = pltpu.roll(low, LANES - 1, 1), pltpu.roll(high, LANES - 1, 1)
            back.append([jnp.where(lane == 0, b, low_r), jnp.where(lane == 0, low_r, high_r)])
            ahead.append(
                [jnp.where(lane == LANES - 1, high_l, low_l), jnp.where(lane == LANES - 1, a, high_l)]
            )
        for h in range(2):
            cols = slice(h * LANES, (h + 1) * LANES)
            c = [q[f][h] for f in range(FIELDS)]
            inner = [st[f, row, at, cols] for f in range(FIELDS)]
            outer = [st[f, row + 2, at, cols] for f in range(FIELDS)]
            above, below = [], []
            for f in range(FIELDS):
                prev = st[f, row + 1, at_dn, cols]
                nxt = st[f, row + 1, at_up, cols]
                below.append(pltpu.roll(jnp.where(sub == SUB - 1, prev, c[f]), 1, 0))
                above.append(pltpu.roll(jnp.where(sub == 0, nxt, c[f]), SUB - 1, 0))
            below[4] = jnp.where(t0 + sub == 0, c[4], below[4])
            above[4] = jnp.where(t0 + sub == tiles * SUB - 1, c[4], above[4])
            inv = 1.0 / c[0]
            v_r, v_p, v_t = c[1] * inv, c[2] * inv, c[3] * inv
            r_up = 0.5 * (v_r + outer[1] / outer[0])
            r_dn = 0.5 * (v_r + inner[1] / inner[0])
            p_up = 0.5 * (v_p + ahead[2][h] / ahead[0][h])
            p_dn = 0.5 * (v_p + back[2][h] / back[0][h])
            t_up_v = jnp.where(t0 + sub == tiles * SUB - 1, 0.0, 0.5 * (v_t + above[3] / above[0]))
            t_dn_v = jnp.where(t0 + sub == 0, 0.0, 0.5 * (v_t + below[3] / below[0]))
            r_up_w, r_dn_w = r_up * w_up, r_dn * w_dn
            for f in range(FIELDS):
                out = c[f]
                out -= r_up_w * jnp.where(r_up > 0, c[f], outer[f]) - r_dn_w * jnp.where(r_dn > 0, inner[f], c[f])
                out -= upwind(t_up_v, c[f], above[f]) - upwind(t_dn_v, below[f], c[f])
                out -= upwind(p_up, c[f], ahead[f][h]) - upwind(p_dn, back[f][h], c[f])
                if f == 1:
                    out -= 0.5 * (0.5 * (0.4 * outer[4] - 0.4 * inner[4]))
                if f == 2:
                    out -= 0.5 * (0.5 * (0.4 * ahead[4][h] - 0.4 * back[4][h]))
                if f == 3:
                    out -= 0.5 * (0.5 * (0.4 * above[4] - 0.4 * below[4]))
                send[row, t, h, f] = out

    def whole_row(row, c):
        lax.fori_loop(0, per, lambda p, _: (compute(row, c * per + p), 0)[1], 0)

    def first_leg(c, row):
        part = send.at[row, pl.ds(c * per, per)]
        return part, whole[c].at[me]

    def produce(c, wanted):
        def step(k, _):
            row = peer(me, k)

            def do():
                whole_row(row, c)
                part, place = first_leg(c, row)

                @pl.when(row != me)
                def _():
                    remote(part, place, s1.at[c], r1.at[c], az=row).start()

                @pl.when(row == me)
                def _():
                    pltpu.make_async_copy(part, place, own1.at[c]).start()

            edge = (row == 0) | (row == rows - 1)
            if wanted == "all":
                do()
            elif wanted == "edge":
                pl.when(edge)(do)
            else:
                pl.when(jnp.logical_not(edge))(do)
            return 0

        lax.fori_loop(0, rows, step, 0)

    right.wait()
    left.wait()
    for c in range(early):
        produce(c, "inside")

    @pl.when(jnp.logical_not(at_inner))
    def _():
        for c in outward:
            c.wait_recv()

    @pl.when(jnp.logical_not(at_outer))
    def _():
        for c in inward:
            c.wait_recv()

    @pl.when(at_inner)
    def _():
        st[:, 0] = st[:, 1]

    @pl.when(at_outer)
    def _():
        st[:, rows + 1] = st[:, rows]

    for c in range(early):
        produce(c, "edge")
    for c in range(early, chunks):
        produce(c, "all")

    amount = amounts[me]
    skip = amount // LANES
    turn = amount % LANES

    def second_leg(c, b):
        thetas = pl.ds(c * per * SUB, per * SUB)
        return turned.at[b, :, thetas], landed.at[me, :, thetas]

    for c in range(chunks):
        wait_bytes(whole[c].at[pl.ds(0, n - 1)], r1.at[c])
        pltpu.make_async_copy(send.at[me, pl.ds(c * per, per)], whole[c].at[me], own1.at[c]).wait()

        def give(k, _, c=c):
            b = peer(me, k)
            for h in range(2):
                a = (2 * b + h - skip) & (2 * n - 1)
                z = (2 * b + h - skip - 1) & (2 * n - 1)
                for p in range(per):
                    for f in range(FIELDS):
                        late = pltpu.roll(whole[c][a // 2, p, a % 2, f], turn, 1)
                        soon = pltpu.roll(whole[c][z // 2, p, z % 2, f], turn, 1)
                        value = jnp.where(lane >= turn, late, soon)
                        turned[b, f, pl.ds((c * per + p) * SUB, SUB), h * LANES : (h + 1) * LANES] = value

            src, dst = second_leg(c, b)

            @pl.when(b != me)
            def _():
                remote(src, dst, s2, r2, az=b).start()

            @pl.when(b == me)
            def _():
                pltpu.make_async_copy(src, dst, own2).start()

            return 0

        lax.fori_loop(0, n, give, 0)

    for c in range(chunks):
        wait_bytes(send.at[pl.ds(0, n - 1), pl.ds(c * per, per)], s1.at[c])
    wait_bytes(landed.at[pl.ds(0, n - 1)], s2)
    wait_bytes(landed.at[me], own2)
    wait_bytes(landed.at[pl.ds(0, n - 1)], r2)

    @pl.when(jnp.logical_not(at_outer))
    def _():
        for c in outward:
            c.wait_send()

    @pl.when(jnp.logical_not(at_inner))
    def _():
        for c in inward:
            c.wait_send()


def deliver(landed, den_o, mom_o, en_o, sems):
    rows = den_o.shape[0]
    parts = sems.shape[0]
    copies = []
    for p in range(parts):
        at = pl.ds(p * (rows // parts), rows // parts)
        copies.append(pltpu.make_async_copy(landed.at[at, 0], den_o.at[at], sems.at[p, 0]))
        for f in range(3):
            copies.append(pltpu.make_async_copy(landed.at[at, 1 + f], mom_o.at[f, at], sems.at[p, 1 + f]))
        copies.append(pltpu.make_async_copy(landed.at[at, 4], en_o.at[at], sems.at[p, 4]))
    for c in copies:
        c.start()
    for c in copies:
        c.wait()


def per_device(density, momenta, energy, shifts):
    rows, thetas, width = density.shape
    n = lax.axis_size("az")
    tiles = thetas // SUB
    chunks, early = 8, 2
    per = tiles // chunks
    dma = pltpu.SemaphoreType.DMA
    f32 = jnp.float32
    hbm = pl.BlockSpec(memory_space=pltpu.HBM)
    landed = pl.pallas_call(
        functools.partial(kernel, chunks, early),
        out_shape=pltpu.VMEM((n, FIELDS, thetas, width), f32),
        in_specs=[hbm] * 4,
        out_specs=pl.BlockSpec(memory_space=pltpu.VMEM),
        scratch_shapes=[
            pltpu.SMEM((rows,), jnp.int32),
            pltpu.VMEM((FIELDS, rows + 2, thetas, width), f32),
            pltpu.VMEM((rows, tiles, 2, FIELDS, SUB, LANES), f32),
            pltpu.VMEM((n, FIELDS, thetas, width), f32),
            pltpu.VMEM((2, tiles, SUB, LANES), f32),
            pltpu.VMEM((2, tiles, SUB, LANES), f32),
            *[pltpu.VMEM((n, per, 2, FIELDS, SUB, LANES), f32) for _ in range(chunks)],
            dma((4,)),
            dma((2, 3)),
            dma((2, 3)),
            dma((2,)),
            dma((2,)),
            dma((chunks,)),
            dma((chunks,)),
            dma((chunks,)),
            dma,
            dma,
            dma,
        ],
        compiler_params=pltpu.CompilerParams(
            collective_id=0, has_side_effects=True, vmem_limit_bytes=56 * 2**20
        ),
        name="transport",
    )(density, momenta, energy, shifts)
    return pl.pallas_call(
        deliver,
        out_shape=[jax.ShapeDtypeStruct(x.shape, f32) for x in (density, momenta, energy)],
        in_specs=[pl.BlockSpec(memory_space=pl.ANY)],
        out_specs=[pl.BlockSpec(memory_space=pl.ANY)] * 3,
        scratch_shapes=[dma((4, FIELDS))],
        compiler_params=pltpu.CompilerParams(vmem_limit_bytes=2**20),
        name="deliver",
    )(landed)


def solution(mesh):
    return jax.shard_map(
        per_device,
        mesh=mesh,
        in_specs=(P("rad", None, "az"), P(None, "rad", None, "az"), P("rad", None, "az"), P("rad")),
        out_specs=(P("rad", None, "az"), P(None, "rad", None, "az"), P("rad", None, "az")),
        check_vma=False,
    )
```

```python
import functools

import jax
import jax.numpy as jnp
from jax import lax
from jax.experimental import pallas as pl
from jax.experimental.pallas import tpu as pltpu
from jax.sharding import PartitionSpec as P

MESH = pl.DeviceIdType.MESH
LANES = 128
SUB = 8
FIELDS = 5


def remote(src, dst, send, recv, **where):
    return pltpu.make_async_remote_copy(
        src_ref=src, dst_ref=dst, send_sem=send, recv_sem=recv, device_id=where, device_id_type=MESH
    )


def wait_bytes(ref, sem):
    pltpu.make_async_copy(ref, ref, sem).wait()


def peer(me, k):
    y = (me // 4 + k // 4) % 4
    x = (me // 2 + k // 2) % 2
    core = (me + k) % 2
    return y * 4 + x * 2 + core


def kernel(chunks, early, den, mom, en, shifts, landed, *refs):
    amounts, st, send, turned, pack, halo, relay = refs[:7]
    whole = refs[7 : 7 + chunks]
    in_sem, shift_sem, rad_send, rad_recv, relay_send, relay_recv, az_send, az_recv, s1, r1, own1, s2, r2, own2 = refs[7 + chunks :]
    rows = den.shape[0]
    tiles = den.shape[1] // SUB
    per = tiles // chunks
    me = lax.axis_index("az")
    n = lax.axis_size("az")
    pos = lax.axis_index("rad")
    groups = lax.axis_size("rad")
    at_inner = pos == 0
    at_outer = pos == groups - 1

    def load(j, first, count):
        at = pl.ds(first * SUB, count * SUB)
        return [
            pltpu.make_async_copy(den.at[:, at], st.at[0, pl.ds(1, rows), at], in_sem.at[j, 0]),
            pltpu.make_async_copy(mom.at[:, :, at], st.at[pl.ds(1, 3), pl.ds(1, rows), at], in_sem.at[j, 1]),
            pltpu.make_async_copy(en.at[:, at], st.at[4, pl.ds(1, rows), at], in_sem.at[j, 2]),
        ]

    loads = [load(0, 0, 2), load(1, 2, tiles - 2)]
    get_shifts = pltpu.make_async_copy(shifts, amounts, shift_sem)
    for part in loads:
        for c in part:
            c.start()
    get_shifts.start()

    barrier = pltpu.get_barrier_semaphore()

    def greet(k, _):
        pl.semaphore_signal(barrier, 1, device_id={"az": peer(me, k)}, device_id_type=MESH)
        return 0

    lax.fori_loop(1, n, greet, 0)

    for j in range(1, groups):
        pl.semaphore_signal(barrier, 1, device_id={"rad": (pos + j) % groups}, device_id_type=MESH)
    pl.semaphore_wait(barrier, n - 1 + groups - 1)

    half = groups // 2
    part_rows = tiles * SUB // half

    def edge_part(row, p):
        at = pl.ds(p * part_rows, part_rows)
        return [den.at[row, at], mom.at[:, row, at], en.at[row, at]]

    def slot_part(slot, p):
        at = pl.ds(p * part_rows, part_rows)
        return [st.at[0, slot, at], st.at[pl.ds(1, 3), slot, at], st.at[4, slot, at]]

    def relay_part():
        return [relay.at[0], relay.at[pl.ds(1, 3)], relay.at[4]]

    def copies(srcs, dsts, send, recv, to):
        return [remote(a, b, send.at[j], recv.at[j], rad=to) for j, (a, b) in enumerate(zip(srcs, dsts))]

    def radial(way, row, slot, to):
        whole_edge = [den.at[row], mom.at[:, row], en.at[row]]
        return copies(whole_edge, [st.at[0, slot], st.at[pl.ds(1, 3), slot], st.at[4, slot]],
                      rad_send.at[way, 0], rad_recv.at[way, 0], to)

    outward = radial(0, rows - 1, 0, (pos + 1) % groups)
    inward = radial(1, 0, rows + 1, (pos + groups - 1) % groups)
    seams = []
    for way, row, slot, source, target, first in ((0, rows - 1, 0, half - 1, half, 0), (1, 0, rows + 1, half, half - 1, half)):
        seam = []
        for p in range(half):
            via = first + p
            final = (slot_part(slot, p), rad_recv.at[way, p], target)
            if via == source:
                seam.append((via, copies(edge_part(row, p), final[0], rad_send.at[way, p], final[1], target), None))
            else:
                to_relay = copies(edge_part(row, p), relay_part(), rad_send.at[way, p], relay_recv, via)
                from_relay = copies(relay_part(), final[0], relay_send, final[1], target)
                seam.append((via, to_relay, from_relay))
        seams.append((source, target, seam))

    has_out = jnp.logical_not(at_outer) & (pos != half - 1)
    has_in = jnp.logical_not(at_inner) & (pos != half)

    @pl.when(has_out)
    def _():
        for c in outward:
            c.start()

    @pl.when(has_in)
    def _():
        for c in inward:
            c.start()

    for source, target, seam in seams:
        @pl.when(pos == source)
        def _():
            for via, leg, _ in seam:
                for c in leg:
                    c.start()

    def forward():
        for source, target, seam in seams:
            for via, leg, onward in seam:
                if onward is not None:
                    @pl.when(pos == via)
                    def _():
                        for a, b in zip(leg, onward):
                            a.wait_recv()
                            b.start()

    def radial_arrived():
        @pl.when(jnp.logical_not(at_inner) & (pos != half))
        def _():
            for c in outward:
                c.wait_recv()

        @pl.when(jnp.logical_not(at_outer) & (pos != half - 1))
        def _():
            for c in inward:
                c.wait_recv()

        for source, target, seam in seams:
            @pl.when(pos == target)
            def _():
                for via, leg, onward in seam:
                    for c in onward or leg:
                        c.wait_recv()

    def radial_sent():
        @pl.when(has_out)
        def _():
            for c in outward:
                c.wait_send()

        @pl.when(has_in)
        def _():
            for c in inward:
                c.wait_send()

        for source, target, seam in seams:
            @pl.when(pos == source)
            def _():
                for via, leg, onward in seam:
                    for c in leg:
                        c.wait_send()

            for via, leg, onward in seam:
                if onward is not None:
                    @pl.when(pos == via)
                    def _():
                        for c in onward:
                            c.wait_send()

    lane = lax.broadcasted_iota(jnp.int32, (SUB, LANES), 1)
    sub = lax.broadcasted_iota(jnp.int32, (SUB, LANES), 0)

    def packing(t, _):
        at = pl.ds(pl.multiple_of(t * SUB, SUB), SUB)
        first = jnp.zeros((SUB, LANES), jnp.float32)
        last = jnp.zeros((SUB, LANES), jnp.float32)
        for f in range(FIELDS):
            for i in range(rows):
                k = f * rows + i
                low = st[f, 1 + i, at, 0:LANES]
                high = st[f, 1 + i, at, LANES : 2 * LANES]
                first = jnp.where(lane == k, pltpu.roll(low, k, 1) if k else low, first)
                last = jnp.where(lane == k, pltpu.roll(high, k + 1, 1), last)
        pack[0, t] = first
        pack[1, t] = last
        return 0

    def edges(j, first, count):
        at = pl.ds(first, count)
        return [
            remote(pack.at[1, at], halo.at[0, at], az_send.at[j, 0], az_recv.at[j, 0], az=(me + 1) % n),
            remote(pack.at[0, at], halo.at[1, at], az_send.at[j, 1], az_recv.at[j, 1], az=(me + n - 1) % n),
        ]

    azimuthal = [edges(0, 0, 1), edges(1, 1, tiles - 1)]
    for c in loads[0]:
        c.wait()
    packing(0, 0)
    for c in azimuthal[0]:
        c.start()
    for c in loads[1]:
        c.wait()
    lax.fori_loop(1, tiles, packing, 0)
    for c in azimuthal[1]:
        c.start()
    get_shifts.wait()

    total = groups * rows

    def radius(index):
        return 1.0 + 2.0 * (index.astype(jnp.float32) + 0.5) / total

    def upwind(face, low, high):
        return face * jnp.where(face > 0, low, high)

    def compute(row, t):
        t0 = pl.multiple_of(t * SUB, SUB)
        at = pl.ds(t0, SUB)
        at_dn = pl.ds(pl.multiple_of(jnp.maximum(t - 1, 0) * SUB, SUB), SUB)
        at_up = pl.ds(pl.multiple_of(jnp.minimum(t + 1, tiles - 1) * SUB, SUB), SUB)
        index = pos * rows + row
        here = radius(index)
        face_up = 0.5 * (here + radius(index + 1))
        face_dn = 0.5 * (radius(index - 1) + here)
        area = jnp.full((SUB, LANES), here * here, jnp.float32)
        w_up = jnp.full((SUB, LANES), face_up * face_up, jnp.float32) / area
        w_dn = jnp.full((SUB, LANES), face_dn * face_dn, jnp.float32) / area
        w_up = jnp.where(index == total - 1, 0.0, w_up)
        w_dn = jnp.where(index == 0, 0.0, w_dn)
        before = halo[0, t]
        after = halo[1, t]
        q = [[st[f, row + 1, at, h * LANES : (h + 1) * LANES] for h in range(2)] for f in range(FIELDS)]
        back, ahead = [], []
        for f in range(FIELDS):
            k = f * rows + row
            b = pltpu.roll(before, (LANES - k) % LANES, 1)
            a = pltpu.roll(after, LANES - 1 - k, 1)
            low, high = q[f]
            low_r, high_r = pltpu.roll(low, 1, 1), pltpu.roll(high, 1, 1)
            low_l, high_l = pltpu.roll(low, LANES - 1, 1), pltpu.roll(high, LANES - 1, 1)
            back.append([jnp.where(lane == 0, b, low_r), jnp.where(lane == 0, low_r, high_r)])
            ahead.append(
                [jnp.where(lane == LANES - 1, high_l, low_l), jnp.where(lane == LANES - 1, a, high_l)]
            )
        for h in range(2):
            cols = slice(h * LANES, (h + 1) * LANES)
            c = [q[f][h] for f in range(FIELDS)]
            inner = [st[f, row, at, cols] for f in range(FIELDS)]
            outer = [st[f, row + 2, at, cols] for f in range(FIELDS)]
            above, below = [], []
            for f in range(FIELDS):
                prev = st[f, row + 1, at_dn, cols]
                nxt = st[f, row + 1, at_up, cols]
                below.append(pltpu.roll(jnp.where(sub == SUB - 1, prev, c[f]), 1, 0))
                above.append(pltpu.roll(jnp.where(sub == 0, nxt, c[f]), SUB - 1, 0))
            below[4] = jnp.where(t0 + sub == 0, c[4], below[4])
            above[4] = jnp.where(t0 + sub == tiles * SUB - 1, c[4], above[4])
            inv = 1.0 / c[0]
            v_r, v_p, v_t = c[1] * inv, c[2] * inv, c[3] * inv
            r_up = 0.5 * (v_r + outer[1] / outer[0])
            r_dn = 0.5 * (v_r + inner[1] / inner[0])
            p_up = 0.5 * (v_p + ahead[2][h] / ahead[0][h])
            p_dn = 0.5 * (v_p + back[2][h] / back[0][h])
            t_up_v = jnp.where(t0 + sub == tiles * SUB - 1, 0.0, 0.5 * (v_t + above[3] / above[0]))
            t_dn_v = jnp.where(t0 + sub == 0, 0.0, 0.5 * (v_t + below[3] / below[0]))
            r_up_w, r_dn_w = r_up * w_up, r_dn * w_dn
            for f in range(FIELDS):
                out = c[f]
                out -= r_up_w * jnp.where(r_up > 0, c[f], outer[f]) - r_dn_w * jnp.where(r_dn > 0, inner[f], c[f])
                out -= upwind(t_up_v, c[f], above[f]) - upwind(t_dn_v, below[f], c[f])
                out -= upwind(p_up, c[f], ahead[f][h]) - upwind(p_dn, back[f][h], c[f])
                if f == 1:
                    out -= 0.5 * (0.5 * (0.4 * outer[4] - 0.4 * inner[4]))
                if f == 2:
                    out -= 0.5 * (0.5 * (0.4 * ahead[4][h] - 0.4 * back[4][h]))
                if f == 3:
                    out -= 0.5 * (0.5 * (0.4 * above[4] - 0.4 * below[4]))
                send[row, t, h, f] = out

    def whole_row(row, c):
        lax.fori_loop(0, per, lambda p, _: (compute(row, c * per + p), 0)[1], 0)

    def first_leg(c, row):
        part = send.at[row, pl.ds(c * per, per)]
        return part, whole[c].at[me]

    def produce(c, wanted):
        def step(k, _):
            row = peer(me, k)

            def do():
                whole_row(row, c)
                part, place = first_leg(c, row)

                @pl.when(row != me)
                def _():
                    remote(part, place, s1.at[c], r1.at[c], az=row).start()

                @pl.when(row == me)
                def _():
                    pltpu.make_async_copy(part, place, own1.at[c]).start()

            edge = (row == 0) | (row == rows - 1)
            if wanted == "all":
                do()
            elif wanted == "edge":
                pl.when(edge)(do)
            else:
                pl.when(jnp.logical_not(edge))(do)
            return 0

        lax.fori_loop(0, rows, step, 0)

    for c in azimuthal[0]:
        c.wait()
    produce(0, "inside")
    forward()
    for c in azimuthal[1]:
        c.wait()
    for c in range(1, early):
        produce(c, "inside")

    radial_arrived()

    @pl.when(at_inner)
    def _():
        st[:, 0] = st[:, 1]

    @pl.when(at_outer)
    def _():
        st[:, rows + 1] = st[:, rows]

    for c in range(early):
        produce(c, "edge")
    for c in range(early, chunks):
        produce(c, "all")

    amount = amounts[me]
    skip = amount // LANES
    turn = amount % LANES

    def second_leg(c, b):
        thetas = pl.ds(c * per * SUB, per * SUB)
        return turned.at[b, :, thetas], landed.at[me, :, thetas]

    for c in range(chunks):
        wait_bytes(whole[c].at[pl.ds(0, n - 1)], r1.at[c])
        pltpu.make_async_copy(send.at[me, pl.ds(c * per, per)], whole[c].at[me], own1.at[c]).wait()

        def give(k, _, c=c):
            b = peer(me, k)
            for h in range(2):
                a = (2 * b + h - skip) & (2 * n - 1)
                z = (2 * b + h - skip - 1) & (2 * n - 1)
                for p in range(per):
                    for f in range(FIELDS):
                        late = pltpu.roll(whole[c][a // 2, p, a % 2, f], turn, 1)
                        soon = pltpu.roll(whole[c][z // 2, p, z % 2, f], turn, 1)
                        value = jnp.where(lane >= turn, late, soon)
                        turned[b, f, pl.ds((c * per + p) * SUB, SUB), h * LANES : (h + 1) * LANES] = value

            src, dst = second_leg(c, b)

            @pl.when(b != me)
            def _():
                remote(src, dst, s2, r2, az=b).start()

            @pl.when(b == me)
            def _():
                pltpu.make_async_copy(src, dst, own2).start()

            return 0

        lax.fori_loop(0, n, give, 0)

    for c in range(chunks):
        wait_bytes(send.at[pl.ds(0, n - 1), pl.ds(c * per, per)], s1.at[c])
    wait_bytes(landed.at[pl.ds(0, n - 1)], s2)
    wait_bytes(landed.at[me], own2)
    wait_bytes(landed.at[pl.ds(0, n - 1)], r2)

    radial_sent()


def deliver(landed, den_o, mom_o, en_o, sems):
    rows = den_o.shape[0]
    parts = sems.shape[0]
    copies = []
    for p in range(parts):
        at = pl.ds(p * (rows // parts), rows // parts)
        copies.append(pltpu.make_async_copy(landed.at[at, 0], den_o.at[at], sems.at[p, 0]))
        for f in range(3):
            copies.append(pltpu.make_async_copy(landed.at[at, 1 + f], mom_o.at[f, at], sems.at[p, 1 + f]))
        copies.append(pltpu.make_async_copy(landed.at[at, 4], en_o.at[at], sems.at[p, 4]))
    for c in copies:
        c.start()
    for c in copies:
        c.wait()


def per_device(density, momenta, energy, shifts):
    rows, thetas, width = density.shape
    n = lax.axis_size("az")
    tiles = thetas // SUB
    chunks, early = 8, 2
    per = tiles // chunks
    half = lax.axis_size("rad") // 2
    dma = pltpu.SemaphoreType.DMA
    f32 = jnp.float32
    hbm = pl.BlockSpec(memory_space=pltpu.HBM)
    landed = pl.pallas_call(
        functools.partial(kernel, chunks, early),
        out_shape=pltpu.VMEM((n, FIELDS, thetas, width), f32),
        in_specs=[hbm] * 4,
        out_specs=pl.BlockSpec(memory_space=pltpu.VMEM),
        scratch_shapes=[
            pltpu.SMEM((rows,), jnp.int32),
            pltpu.VMEM((FIELDS, rows + 2, thetas, width), f32),
            pltpu.VMEM((rows, tiles, 2, FIELDS, SUB, LANES), f32),
            pltpu.VMEM((n, FIELDS, thetas, width), f32),
            pltpu.VMEM((2, tiles, SUB, LANES), f32),
            pltpu.VMEM((2, tiles, SUB, LANES), f32),
            pltpu.VMEM((FIELDS, 2 * thetas // lax.axis_size("rad"), width), f32),
            *[pltpu.VMEM((n, per, 2, FIELDS, SUB, LANES), f32) for _ in range(chunks)],
            dma((2, 3)),
            dma,
            dma((2, half, 3)),
            dma((2, half, 3)),
            dma((3,)),
            dma((3,)),
            dma((2, 2)),
            dma((2, 2)),
            dma((chunks,)),
            dma((chunks,)),
            dma((chunks,)),
            dma,
            dma,
            dma,
        ],
        compiler_params=pltpu.CompilerParams(
            collective_id=0, has_side_effects=True, vmem_limit_bytes=56 * 2**20
        ),
        name="transport",
    )(density, momenta, energy, shifts)
    return pl.pallas_call(
        deliver,
        out_shape=[jax.ShapeDtypeStruct(x.shape, f32) for x in (density, momenta, energy)],
        in_specs=[pl.BlockSpec(memory_space=pl.ANY)],
        out_specs=[pl.BlockSpec(memory_space=pl.ANY)] * 3,
        scratch_shapes=[dma((4, FIELDS))],
        compiler_params=pltpu.CompilerParams(vmem_limit_bytes=2**20),
        name="deliver",
    )(landed)


def solution(mesh):
    return jax.shard_map(
        per_device,
        mesh=mesh,
        in_specs=(P("rad", None, "az"), P(None, "rad", None, "az"), P("rad", None, "az"), P("rad")),
        out_specs=(P("rad", None, "az"), P(None, "rad", None, "az"), P("rad", None, "az")),
        check_vma=False,
    )
```

```python
import functools

import jax
import jax.numpy as jnp
from jax import lax
from jax.experimental import pallas as pl
from jax.experimental.pallas import tpu as pltpu
from jax.sharding import PartitionSpec as P

MESH = pl.DeviceIdType.MESH
LANES = 128
SUB = 8
FIELDS = 5


def remote(src, dst, send, recv, **where):
    return pltpu.make_async_remote_copy(
        src_ref=src, dst_ref=dst, send_sem=send, recv_sem=recv, device_id=where, device_id_type=MESH
    )


def wait_bytes(ref, sem):
    pltpu.make_async_copy(ref, ref, sem).wait()


def peer(me, k):
    y = (me // 4 + k // 4) % 4
    x = (me // 2 + k // 2) % 2
    core = (me + k) % 2
    return y * 4 + x * 2 + core


def kernel(chunks, early, den, mom, en, shifts, landed, *refs):
    amounts, st, send, turned, pack, halo, relay = refs[:7]
    whole = refs[7 : 7 + chunks]
    in_sem, shift_sem, rad_send, rad_recv, relay_send, relay_recv, az_send, az_recv, s1, r1, own1, s2, r2, own2 = refs[7 + chunks :]
    rows = den.shape[0]
    tiles = den.shape[1] // SUB
    per = tiles // chunks
    me = lax.axis_index("az")
    n = lax.axis_size("az")
    pos = lax.axis_index("rad")
    groups = lax.axis_size("rad")
    at_inner = pos == 0
    at_outer = pos == groups - 1

    def load(j, first, count):
        at = pl.ds(first * SUB, count * SUB)
        return [
            pltpu.make_async_copy(den.at[:, at], st.at[0, pl.ds(1, rows), at], in_sem.at[j, 0]),
            pltpu.make_async_copy(mom.at[:, :, at], st.at[pl.ds(1, 3), pl.ds(1, rows), at], in_sem.at[j, 1]),
            pltpu.make_async_copy(en.at[:, at], st.at[4, pl.ds(1, rows), at], in_sem.at[j, 2]),
        ]

    loads = [load(0, 0, 2), load(1, 2, tiles - 2)]
    get_shifts = pltpu.make_async_copy(shifts, amounts, shift_sem)
    for part in loads:
        for c in part:
            c.start()
    get_shifts.start()

    barrier = pltpu.get_barrier_semaphore()

    def greet(k, _):
        pl.semaphore_signal(barrier, 1, device_id={"az": peer(me, k)}, device_id_type=MESH)
        return 0

    lax.fori_loop(1, n, greet, 0)

    half = groups // 2
    across = (pos + half) % groups
    has_out = jnp.logical_not(at_outer) & (pos != half - 1)
    has_in = jnp.logical_not(at_inner) & (pos != half)
    pl.semaphore_signal(barrier, 1, device_id={"rad": across}, device_id_type=MESH)

    @pl.when(has_out)
    def _():
        pl.semaphore_signal(barrier, 1, device_id={"rad": pos + 1}, device_id_type=MESH)

    @pl.when(has_in)
    def _():
        pl.semaphore_signal(barrier, 1, device_id={"rad": pos - 1}, device_id_type=MESH)

    pl.semaphore_wait(barrier, n + jnp.where(has_out, 1, 0) + jnp.where(has_in, 1, 0))

    def radial(way, row, slot, to):
        srcs = [den.at[row], mom.at[:, row], en.at[row]]
        dsts = [st.at[0, slot], st.at[pl.ds(1, 3), slot], st.at[4, slot]]
        return [remote(a, b, rad_send.at[way, j], rad_recv.at[way, j], rad=to) for j, (a, b) in enumerate(zip(srcs, dsts))]

    outward = radial(0, rows - 1, 0, (pos + 1) % groups)
    inward = radial(1, 0, rows + 1, (pos + groups - 1) % groups)

    @pl.when(has_out)
    def _():
        for c in outward:
            c.start()

    @pl.when(has_in)
    def _():
        for c in inward:
            c.start()

    part_rows = tiles * SUB // half
    low = pos < half
    place = pos % half

    def seam_part(way, p):
        carries = jnp.where(low, p <= place, p >= place)
        crossing = low if way == 0 else jnp.logical_not(low)
        step = groups - 1 if way == 0 else 1
        to = jnp.where(crossing & (p == place), across, (pos + step) % groups)
        last = pos == (half if way == 0 else half - 1)
        at = pl.ds(p * part_rows, part_rows)
        edge = st.at[:, rows if way == 0 else 1, at]

        def copy(src):
            return remote(src, relay.at[way, p], relay_send.at[way, p], relay_recv.at[way, p], rad=to)

        return carries, carries & jnp.logical_not(last), copy, edge

    def seam(stage):
        for way in range(2):
            hops = jnp.where(low, half - 1 - place, half - place) if way == 0 else jnp.where(low, place + 1, place)

            @pl.when(hops == stage)
            def _():
                for p in range(half):
                    carries, hands_on, copy, edge = seam_part(way, p)
                    if stage == 0:
                        @pl.when(carries)
                        def _():
                            copy(edge).start()
                    else:
                        @pl.when(carries)
                        def _():
                            copy(relay.at[way, p]).wait_recv()

                        @pl.when(hands_on)
                        def _():
                            copy(relay.at[way, p]).start()

    def seam_into_state():
        for way in range(2):
            @pl.when(pos == (half if way == 0 else half - 1))
            def _():
                for p in range(half):
                    st[:, 0 if way == 0 else rows + 1, p * part_rows : (p + 1) * part_rows] = relay[way, p]

    def radial_arrived():
        @pl.when(has_in)
        def _():
            for c in outward:
                c.wait_recv()

        @pl.when(has_out)
        def _():
            for c in inward:
                c.wait_recv()

        @pl.when(at_inner)
        def _():
            st[:, 0] = st[:, 1]

        @pl.when(at_outer)
        def _():
            st[:, rows + 1] = st[:, rows]

    def radial_sent():
        @pl.when(has_out)
        def _():
            for c in outward:
                c.wait_send()

        @pl.when(has_in)
        def _():
            for c in inward:
                c.wait_send()

        for way in range(2):
            for p in range(half):
                carries, hands_on, copy, edge = seam_part(way, p)

                @pl.when(hands_on)
                def _():
                    copy(relay.at[way, p]).wait_send()

    lane = lax.broadcasted_iota(jnp.int32, (SUB, LANES), 1)
    sub = lax.broadcasted_iota(jnp.int32, (SUB, LANES), 0)

    def packing(t, _):
        at = pl.ds(pl.multiple_of(t * SUB, SUB), SUB)
        first = jnp.zeros((SUB, LANES), jnp.float32)
        last = jnp.zeros((SUB, LANES), jnp.float32)
        for f in range(FIELDS):
            for i in range(rows):
                k = f * rows + i
                low = st[f, 1 + i, at, 0:LANES]
                high = st[f, 1 + i, at, LANES : 2 * LANES]
                first = jnp.where(lane == k, pltpu.roll(low, k, 1) if k else low, first)
                last = jnp.where(lane == k, pltpu.roll(high, k + 1, 1), last)
        pack[0, t] = first
        pack[1, t] = last
        return 0

    def edges(j, first, count):
        at = pl.ds(first, count)
        return [
            remote(pack.at[1, at], halo.at[0, at], az_send.at[j, 0], az_recv.at[j, 0], az=(me + 1) % n),
            remote(pack.at[0, at], halo.at[1, at], az_send.at[j, 1], az_recv.at[j, 1], az=(me + n - 1) % n),
        ]

    azimuthal = [edges(0, 0, 1), edges(1, 1, tiles - 1)]
    for c in loads[0]:
        c.wait()
    packing(0, 0)
    for c in azimuthal[0]:
        c.start()
    for c in loads[1]:
        c.wait()
    seam(0)
    lax.fori_loop(1, tiles, packing, 0)
    for c in azimuthal[1]:
        c.start()
    get_shifts.wait()

    total = groups * rows

    def radius(index):
        return 1.0 + 2.0 * (index.astype(jnp.float32) + 0.5) / total

    def upwind(face, low, high):
        return face * jnp.where(face > 0, low, high)

    def compute(row, t):
        t0 = pl.multiple_of(t * SUB, SUB)
        at = pl.ds(t0, SUB)
        at_dn = pl.ds(pl.multiple_of(jnp.maximum(t - 1, 0) * SUB, SUB), SUB)
        at_up = pl.ds(pl.multiple_of(jnp.minimum(t + 1, tiles - 1) * SUB, SUB), SUB)
        index = pos * rows + row
        here = radius(index)
        face_up = 0.5 * (here + radius(index + 1))
        face_dn = 0.5 * (radius(index - 1) + here)
        area = jnp.full((SUB, LANES), here * here, jnp.float32)
        w_up = jnp.full((SUB, LANES), face_up * face_up, jnp.float32) / area
        w_dn = jnp.full((SUB, LANES), face_dn * face_dn, jnp.float32) / area
        w_up = jnp.where(index == total - 1, 0.0, w_up)
        w_dn = jnp.where(index == 0, 0.0, w_dn)
        before = halo[0, t]
        after = halo[1, t]
        q = [[st[f, row + 1, at, h * LANES : (h + 1) * LANES] for h in range(2)] for f in range(FIELDS)]
        back, ahead = [], []
        for f in range(FIELDS):
            k = f * rows + row
            b = pltpu.roll(before, (LANES - k) % LANES, 1)
            a = pltpu.roll(after, LANES - 1 - k, 1)
            low, high = q[f]
            low_r, high_r = pltpu.roll(low, 1, 1), pltpu.roll(high, 1, 1)
            low_l, high_l = pltpu.roll(low, LANES - 1, 1), pltpu.roll(high, LANES - 1, 1)
            back.append([jnp.where(lane == 0, b, low_r), jnp.where(lane == 0, low_r, high_r)])
            ahead.append(
                [jnp.where(lane == LANES - 1, high_l, low_l), jnp.where(lane == LANES - 1, a, high_l)]
            )
        for h in range(2):
            cols = slice(h * LANES, (h + 1) * LANES)
            c = [q[f][h] for f in range(FIELDS)]
            inner = [st[f, row, at, cols] for f in range(FIELDS)]
            outer = [st[f, row + 2, at, cols] for f in range(FIELDS)]
            above, below = [], []
            for f in range(FIELDS):
                prev = st[f, row + 1, at_dn, cols]
                nxt = st[f, row + 1, at_up, cols]
                below.append(pltpu.roll(jnp.where(sub == SUB - 1, prev, c[f]), 1, 0))
                above.append(pltpu.roll(jnp.where(sub == 0, nxt, c[f]), SUB - 1, 0))
            below[4] = jnp.where(t0 + sub == 0, c[4], below[4])
            above[4] = jnp.where(t0 + sub == tiles * SUB - 1, c[4], above[4])
            inv = 1.0 / c[0]
            v_r, v_p, v_t = c[1] * inv, c[2] * inv, c[3] * inv
            r_up = 0.5 * (v_r + outer[1] / outer[0])
            r_dn = 0.5 * (v_r + inner[1] / inner[0])
            p_up = 0.5 * (v_p + ahead[2][h] / ahead[0][h])
            p_dn = 0.5 * (v_p + back[2][h] / back[0][h])
            t_up_v = jnp.where(t0 + sub == tiles * SUB - 1, 0.0, 0.5 * (v_t + above[3] / above[0]))
            t_dn_v = jnp.where(t0 + sub == 0, 0.0, 0.5 * (v_t + below[3] / below[0]))
            r_up_w, r_dn_w = r_up * w_up, r_dn * w_dn
            for f in range(FIELDS):
                out = c[f]
                out -= r_up_w * jnp.where(r_up > 0, c[f], outer[f]) - r_dn_w * jnp.where(r_dn > 0, inner[f], c[f])
                out -= upwind(t_up_v, c[f], above[f]) - upwind(t_dn_v, below[f], c[f])
                out -= upwind(p_up, c[f], ahead[f][h]) - upwind(p_dn, back[f][h], c[f])
                if f == 1:
                    out -= 0.5 * (0.5 * (0.4 * outer[4] - 0.4 * inner[4]))
                if f == 2:
                    out -= 0.5 * (0.5 * (0.4 * ahead[4][h] - 0.4 * back[4][h]))
                if f == 3:
                    out -= 0.5 * (0.5 * (0.4 * above[4] - 0.4 * below[4]))
                send[row, t, h, f] = out

    def whole_row(row, c):
        lax.fori_loop(0, per, lambda p, _: (compute(row, c * per + p), 0)[1], 0)

    def turn_of(c):
        return c * rows // early % rows

    def first_leg(c, row):
        part = send.at[row, pl.ds(c * per, per)]
        return part, whole[c].at[me]

    def produce(c, wanted):
        def step(k, _):
            to = peer(me, k)
            row = (to + n - turn_of(c)) % n

            def do():
                whole_row(row, c)
                part, place = first_leg(c, row)

                @pl.when(to != me)
                def _():
                    remote(part, place, s1.at[c], r1.at[c], az=to).start()

                @pl.when(to == me)
                def _():
                    pltpu.make_async_copy(part, place, own1.at[c]).start()

            edge = (row == 0) | (row == rows - 1)
            if wanted == "every":
                do()
            elif wanted == "edges":
                pl.when(edge)(do)
            else:
                pl.when(jnp.logical_not(edge))(do)
            return 0

        lax.fori_loop(0, rows, step, 0)

    for c in azimuthal[0]:
        c.wait()
    for c in range(chunks):
        produce(c, "inside" if c < early else "every")
        if c == 0:
            for a in azimuthal[1]:
                a.wait()
        if c < half:
            seam(c + 1)
        if c == early - 1:
            radial_arrived()
            seam_into_state()
            for e in range(early):
                produce(e, "edges")

    def second_leg(c, b):
        thetas = pl.ds(c * per * SUB, per * SUB)
        return turned.at[b, :, thetas], landed.at[(me + n - turn_of(c)) % n, :, thetas]

    for c in range(chunks):
        wait_bytes(whole[c].at[pl.ds(0, n - 1)], r1.at[c])
        pltpu.make_async_copy(send.at[me, pl.ds(c * per, per)], whole[c].at[me], own1.at[c]).wait()

        amount = amounts[(me + n - turn_of(c)) % n]
        skip = amount // LANES
        turn = amount % LANES

        def give(k, _, c=c, skip=skip, turn=turn):
            b = peer(me, k)
            for h in range(2):
                a = (2 * b + h - skip) & (2 * n - 1)
                z = (2 * b + h - skip - 1) & (2 * n - 1)
                for p in range(per):
                    for f in range(FIELDS):
                        late = pltpu.roll(whole[c][a // 2, p, a % 2, f], turn, 1)
                        soon = pltpu.roll(whole[c][z // 2, p, z % 2, f], turn, 1)
                        value = jnp.where(lane >= turn, late, soon)
                        turned[b, f, pl.ds((c * per + p) * SUB, SUB), h * LANES : (h + 1) * LANES] = value

            src, dst = second_leg(c, b)

            @pl.when(b != me)
            def _():
                remote(src, dst, s2, r2, az=b).start()

            @pl.when(b == me)
            def _():
                pltpu.make_async_copy(src, dst, own2).start()

            return 0

        lax.fori_loop(0, n, give, 0)

    for c in range(chunks):
        wait_bytes(send.at[pl.ds(0, n - 1), pl.ds(c * per, per)], s1.at[c])
    wait_bytes(landed.at[pl.ds(0, n - 1)], s2)
    wait_bytes(landed.at[me], own2)
    wait_bytes(landed.at[pl.ds(0, n - 1)], r2)

    radial_sent()


def deliver(landed, den_o, mom_o, en_o, sems):
    rows = den_o.shape[0]
    parts = sems.shape[0]
    copies = []
    for p in range(parts):
        at = pl.ds(p * (rows // parts), rows // parts)
        copies.append(pltpu.make_async_copy(landed.at[at, 0], den_o.at[at], sems.at[p, 0]))
        for f in range(3):
            copies.append(pltpu.make_async_copy(landed.at[at, 1 + f], mom_o.at[f, at], sems.at[p, 1 + f]))
        copies.append(pltpu.make_async_copy(landed.at[at, 4], en_o.at[at], sems.at[p, 4]))
    for c in copies:
        c.start()
    for c in copies:
        c.wait()


def per_device(density, momenta, energy, shifts):
    rows, thetas, width = density.shape
    n = lax.axis_size("az")
    tiles = thetas // SUB
    chunks, early = 8, 4
    per = tiles // chunks
    half = lax.axis_size("rad") // 2
    dma = pltpu.SemaphoreType.DMA
    f32 = jnp.float32
    hbm = pl.BlockSpec(memory_space=pltpu.HBM)
    landed = pl.pallas_call(
        functools.partial(kernel, chunks, early),
        out_shape=pltpu.VMEM((n, FIELDS, thetas, width), f32),
        in_specs=[hbm] * 4,
        out_specs=pl.BlockSpec(memory_space=pltpu.VMEM),
        scratch_shapes=[
            pltpu.SMEM((rows,), jnp.int32),
            pltpu.VMEM((FIELDS, rows + 2, thetas, width), f32),
            pltpu.VMEM((rows, tiles, 2, FIELDS, SUB, LANES), f32),
            pltpu.VMEM((n, FIELDS, thetas, width), f32),
            pltpu.VMEM((2, tiles, SUB, LANES), f32),
            pltpu.VMEM((2, tiles, SUB, LANES), f32),
            pltpu.VMEM((2, half, FIELDS, thetas // half, width), f32),
            *[pltpu.VMEM((n, per, 2, FIELDS, SUB, LANES), f32) for _ in range(chunks)],
            dma((2, 3)),
            dma,
            dma((2, 3)),
            dma((2, 3)),
            dma((2, half)),
            dma((2, half)),
            dma((2, 2)),
            dma((2, 2)),
            dma((chunks,)),
            dma((chunks,)),
            dma((chunks,)),
            dma,
            dma,
            dma,
        ],
        compiler_params=pltpu.CompilerParams(
            collective_id=0, has_side_effects=True, vmem_limit_bytes=56 * 2**20
        ),
        name="transport",
    )(density, momenta, energy, shifts)
    return pl.pallas_call(
        deliver,
        out_shape=[jax.ShapeDtypeStruct(x.shape, f32) for x in (density, momenta, energy)],
        in_specs=[pl.BlockSpec(memory_space=pl.ANY)],
        out_specs=[pl.BlockSpec(memory_space=pl.ANY)] * 3,
        scratch_shapes=[dma((4, FIELDS))],
        compiler_params=pltpu.CompilerParams(vmem_limit_bytes=2**20),
        name="deliver",
    )(landed)


def solution(mesh):
    return jax.shard_map(
        per_device,
        mesh=mesh,
        in_specs=(P("rad", None, "az"), P(None, "rad", None, "az"), P("rad", None, "az"), P("rad")),
        out_specs=(P("rad", None, "az"), P(None, "rad", None, "az"), P("rad", None, "az")),
        check_vma=False,
    )
```

```python
import functools

import jax
import jax.numpy as jnp
from jax import lax
from jax.experimental import pallas as pl
from jax.experimental.pallas import tpu as pltpu
from jax.sharding import PartitionSpec as P

MESH = pl.DeviceIdType.MESH
LANES = 128
SUB = 8
FIELDS = 5


def remote(src, dst, send, recv, **where):
    return pltpu.make_async_remote_copy(
        src_ref=src, dst_ref=dst, send_sem=send, recv_sem=recv, device_id=where, device_id_type=MESH
    )


def wait_bytes(ref, sem):
    pltpu.make_async_copy(ref, ref, sem).wait()


def peer(me, k):
    y = (me // 4 + k // 4) % 4
    x = (me // 2 + k // 2) % 2
    core = (me + k) % 2
    return y * 4 + x * 2 + core


def kernel(chunks, early, den, mom, en, shifts, landed, *refs):
    amounts, st, send, turned, pack, halo, relay = refs[:7]
    whole = refs[7 : 7 + chunks]
    in_sem, shift_sem, rad_send, rad_recv, relay_send, relay_recv, az_send, az_recv, s1, r1, own1, s2, r2, own2 = refs[7 + chunks :]
    rows = den.shape[0]
    tiles = den.shape[1] // SUB
    per = tiles // chunks
    me = lax.axis_index("az")
    n = lax.axis_size("az")
    pos = lax.axis_index("rad")
    groups = lax.axis_size("rad")
    at_inner = pos == 0
    at_outer = pos == groups - 1

    def load(j, first, count):
        at = pl.ds(first * SUB, count * SUB)
        return [
            pltpu.make_async_copy(den.at[:, at], st.at[0, pl.ds(1, rows), at], in_sem.at[j, 0]),
            pltpu.make_async_copy(mom.at[:, :, at], st.at[pl.ds(1, 3), pl.ds(1, rows), at], in_sem.at[j, 1]),
            pltpu.make_async_copy(en.at[:, at], st.at[4, pl.ds(1, rows), at], in_sem.at[j, 2]),
        ]

    loads = [load(0, 0, 2), load(1, 2, tiles - 2)]
    get_shifts = pltpu.make_async_copy(shifts, amounts, shift_sem)
    for part in loads:
        for c in part:
            c.start()
    get_shifts.start()

    barrier = pltpu.get_barrier_semaphore()

    def greet(k, _):
        pl.semaphore_signal(barrier, 1, device_id={"az": peer(me, k)}, device_id_type=MESH)
        return 0

    lax.fori_loop(1, n, greet, 0)

    half = groups // 2
    across = (pos + half) % groups
    has_out = jnp.logical_not(at_outer) & (pos != half - 1)
    has_in = jnp.logical_not(at_inner) & (pos != half)
    pl.semaphore_signal(barrier, 1, device_id={"rad": across}, device_id_type=MESH)

    @pl.when(has_out)
    def _():
        pl.semaphore_signal(barrier, 1, device_id={"rad": pos + 1}, device_id_type=MESH)

    @pl.when(has_in)
    def _():
        pl.semaphore_signal(barrier, 1, device_id={"rad": pos - 1}, device_id_type=MESH)

    pl.semaphore_wait(barrier, n + jnp.where(has_out, 1, 0) + jnp.where(has_in, 1, 0))

    def radial(way, row, slot, to):
        srcs = [den.at[row], mom.at[:, row], en.at[row]]
        dsts = [st.at[0, slot], st.at[pl.ds(1, 3), slot], st.at[4, slot]]
        return [remote(a, b, rad_send.at[way, j], rad_recv.at[way, j], rad=to) for j, (a, b) in enumerate(zip(srcs, dsts))]

    outward = radial(0, rows - 1, 0, (pos + 1) % groups)
    inward = radial(1, 0, rows + 1, (pos + groups - 1) % groups)

    part_rows = tiles * SUB // half
    low = pos < half
    place = pos % half

    def seam_part(way, p):
        carries = jnp.where(low, p <= place, p >= place)
        crossing = low if way == 0 else jnp.logical_not(low)
        step = groups - 1 if way == 0 else 1
        to = jnp.where(crossing & (p == place), across, (pos + step) % groups)
        last = pos == (half if way == 0 else half - 1)
        at = pl.ds(p * part_rows, part_rows)
        row = rows - 1 if way == 0 else 0
        edge = [den.at[row, at], mom.at[:, row, at], en.at[row, at]]
        slot = [relay.at[way, p, 0], relay.at[way, p, pl.ds(1, 3)], relay.at[way, p, 4]]

        def copy(src, dst):
            return remote(src, dst, relay_send.at[way, p], relay_recv.at[way, p], rad=to)

        first = [copy(a, b) for a, b in zip(edge, slot)]
        return carries, carries & jnp.logical_not(last), copy(relay.at[way, p], relay.at[way, p]), first

    def seam(stage):
        for way in range(2):
            hops = jnp.where(low, half - 1 - place, half - place) if way == 0 else jnp.where(low, place + 1, place)

            @pl.when(hops == stage)
            def _():
                for p in range(half):
                    carries, hands_on, onward, first = seam_part(way, p)
                    if stage == 0:
                        @pl.when(carries)
                        def _():
                            for a in first:
                                a.start()
                    else:
                        @pl.when(carries)
                        def _():
                            onward.wait_recv()

                        @pl.when(hands_on)
                        def _():
                            onward.start()

    seam(0)

    @pl.when(has_out)
    def _():
        for c in outward:
            c.start()

    @pl.when(has_in)
    def _():
        for c in inward:
            c.start()

    def seam_into_state():
        for way in range(2):
            @pl.when(pos == (half if way == 0 else half - 1))
            def _():
                for p in range(half):
                    st[:, 0 if way == 0 else rows + 1, p * part_rows : (p + 1) * part_rows] = relay[way, p]

    def radial_arrived():
        @pl.when(has_in)
        def _():
            for c in outward:
                c.wait_recv()

        @pl.when(has_out)
        def _():
            for c in inward:
                c.wait_recv()

        @pl.when(at_inner)
        def _():
            st[:, 0] = st[:, 1]

        @pl.when(at_outer)
        def _():
            st[:, rows + 1] = st[:, rows]

    def radial_sent():
        @pl.when(has_out)
        def _():
            for c in outward:
                c.wait_send()

        @pl.when(has_in)
        def _():
            for c in inward:
                c.wait_send()

        for way in range(2):
            for p in range(half):
                carries, hands_on, onward, first = seam_part(way, p)

                @pl.when(hands_on)
                def _():
                    onward.wait_send()

    lane = lax.broadcasted_iota(jnp.int32, (SUB, LANES), 1)
    sub = lax.broadcasted_iota(jnp.int32, (SUB, LANES), 0)

    def packing(t, _):
        at = pl.ds(pl.multiple_of(t * SUB, SUB), SUB)
        first = jnp.zeros((SUB, LANES), jnp.float32)
        last = jnp.zeros((SUB, LANES), jnp.float32)
        for f in range(FIELDS):
            for i in range(rows):
                k = f * rows + i
                low = st[f, 1 + i, at, 0:LANES]
                high = st[f, 1 + i, at, LANES : 2 * LANES]
                first = jnp.where(lane == k, pltpu.roll(low, k, 1) if k else low, first)
                last = jnp.where(lane == k, pltpu.roll(high, k + 1, 1), last)
        pack[0, t] = first
        pack[1, t] = last
        return 0

    def edges(j, first, count):
        at = pl.ds(first, count)
        return [
            remote(pack.at[1, at], halo.at[0, at], az_send.at[j, 0], az_recv.at[j, 0], az=(me + 1) % n),
            remote(pack.at[0, at], halo.at[1, at], az_send.at[j, 1], az_recv.at[j, 1], az=(me + n - 1) % n),
        ]

    azimuthal = [edges(0, 0, 1), edges(1, 1, tiles - 1)]
    for c in loads[0]:
        c.wait()
    packing(0, 0)
    for c in azimuthal[0]:
        c.start()
    for c in loads[1]:
        c.wait()
    lax.fori_loop(1, tiles, packing, 0)
    for c in azimuthal[1]:
        c.start()
    get_shifts.wait()

    total = groups * rows

    def radius(index):
        return 1.0 + 2.0 * (index.astype(jnp.float32) + 0.5) / total

    def upwind(face, low, high):
        return face * jnp.where(face > 0, low, high)

    def compute(row, t):
        t0 = pl.multiple_of(t * SUB, SUB)
        at = pl.ds(t0, SUB)
        at_dn = pl.ds(pl.multiple_of(jnp.maximum(t - 1, 0) * SUB, SUB), SUB)
        at_up = pl.ds(pl.multiple_of(jnp.minimum(t + 1, tiles - 1) * SUB, SUB), SUB)
        index = pos * rows + row
        here = radius(index)
        face_up = 0.5 * (here + radius(index + 1))
        face_dn = 0.5 * (radius(index - 1) + here)
        area = jnp.full((SUB, LANES), here * here, jnp.float32)
        w_up = jnp.full((SUB, LANES), face_up * face_up, jnp.float32) / area
        w_dn = jnp.full((SUB, LANES), face_dn * face_dn, jnp.float32) / area
        w_up = jnp.where(index == total - 1, 0.0, w_up)
        w_dn = jnp.where(index == 0, 0.0, w_dn)
        before = halo[0, t]
        after = halo[1, t]
        q = [[st[f, row + 1, at, h * LANES : (h + 1) * LANES] for h in range(2)] for f in range(FIELDS)]
        back, ahead = [], []
        for f in range(FIELDS):
            k = f * rows + row
            b = pltpu.roll(before, (LANES - k) % LANES, 1)
            a = pltpu.roll(after, LANES - 1 - k, 1)
            low, high = q[f]
            low_r, high_r = pltpu.roll(low, 1, 1), pltpu.roll(high, 1, 1)
            low_l, high_l = pltpu.roll(low, LANES - 1, 1), pltpu.roll(high, LANES - 1, 1)
            back.append([jnp.where(lane == 0, b, low_r), jnp.where(lane == 0, low_r, high_r)])
            ahead.append(
                [jnp.where(lane == LANES - 1, high_l, low_l), jnp.where(lane == LANES - 1, a, high_l)]
            )
        for h in range(2):
            cols = slice(h * LANES, (h + 1) * LANES)
            c = [q[f][h] for f in range(FIELDS)]
            inner = [st[f, row, at, cols] for f in range(FIELDS)]
            outer = [st[f, row + 2, at, cols] for f in range(FIELDS)]
            above, below = [], []
            for f in range(FIELDS):
                prev = st[f, row + 1, at_dn, cols]
                nxt = st[f, row + 1, at_up, cols]
                below.append(pltpu.roll(jnp.where(sub == SUB - 1, prev, c[f]), 1, 0))
                above.append(pltpu.roll(jnp.where(sub == 0, nxt, c[f]), SUB - 1, 0))
            below[4] = jnp.where(t0 + sub == 0, c[4], below[4])
            above[4] = jnp.where(t0 + sub == tiles * SUB - 1, c[4], above[4])
            inv = 1.0 / c[0]
            v_r, v_p, v_t = c[1] * inv, c[2] * inv, c[3] * inv
            r_up = 0.5 * (v_r + outer[1] / outer[0])
            r_dn = 0.5 * (v_r + inner[1] / inner[0])
            p_up = 0.5 * (v_p + ahead[2][h] / ahead[0][h])
            p_dn = 0.5 * (v_p + back[2][h] / back[0][h])
            t_up_v = jnp.where(t0 + sub == tiles * SUB - 1, 0.0, 0.5 * (v_t + above[3] / above[0]))
            t_dn_v = jnp.where(t0 + sub == 0, 0.0, 0.5 * (v_t + below[3] / below[0]))
            r_up_w, r_dn_w = r_up * w_up, r_dn * w_dn
            for f in range(FIELDS):
                out = c[f]
                out -= r_up_w * jnp.where(r_up > 0, c[f], outer[f]) - r_dn_w * jnp.where(r_dn > 0, inner[f], c[f])
                out -= upwind(t_up_v, c[f], above[f]) - upwind(t_dn_v, below[f], c[f])
                out -= upwind(p_up, c[f], ahead[f][h]) - upwind(p_dn, back[f][h], c[f])
                if f == 1:
                    out -= 0.5 * (0.5 * (0.4 * outer[4] - 0.4 * inner[4]))
                if f == 2:
                    out -= 0.5 * (0.5 * (0.4 * ahead[4][h] - 0.4 * back[4][h]))
                if f == 3:
                    out -= 0.5 * (0.5 * (0.4 * above[4] - 0.4 * below[4]))
                send[row, t, h, f] = out

    def whole_row(row, c):
        lax.fori_loop(0, per, lambda p, _: (compute(row, c * per + p), 0)[1], 0)

    def turn_of(c):
        return (c % 2 * 4 + c // 2 % 2 * 2 + c // 4) * (rows // 8) % rows

    def first_leg(c, row):
        part = send.at[row, pl.ds(c * per, per)]
        return part, whole[c].at[me]

    def produce(c, wanted):
        def step(k, _):
            to = peer(me, k)
            row = (to + n - turn_of(c)) % n

            def do():
                whole_row(row, c)
                part, place = first_leg(c, row)

                @pl.when(to != me)
                def _():
                    remote(part, place, s1.at[c], r1.at[c], az=to).start()

                @pl.when(to == me)
                def _():
                    pltpu.make_async_copy(part, place, own1.at[c]).start()

            edge = (row == 0) | (row == rows - 1)
            if wanted == "every":
                do()
            elif wanted == "edges":
                pl.when(edge)(do)
            else:
                pl.when(jnp.logical_not(edge))(do)
            return 0

        lax.fori_loop(0, rows, step, 0)

    for c in azimuthal[0]:
        c.wait()
    for c in range(chunks):
        produce(c, "inside" if c < early else "every")
        if c == 0:
            for a in azimuthal[1]:
                a.wait()
        if 1 <= c - early + half + 1 <= half:
            seam(c - early + half + 1)
        if c == early - 1:
            radial_arrived()
            seam_into_state()
            for e in range(early):
                produce(e, "edges")

    def second_leg(c, b):
        thetas = pl.ds(c * per * SUB, per * SUB)
        return turned.at[b, :, thetas], landed.at[(me + n - turn_of(c)) % n, :, thetas]

    for c in range(chunks):
        wait_bytes(whole[c].at[pl.ds(0, n - 1)], r1.at[c])
        pltpu.make_async_copy(send.at[me, pl.ds(c * per, per)], whole[c].at[me], own1.at[c]).wait()

        amount = amounts[(me + n - turn_of(c)) % n]
        skip = amount // LANES
        turn = amount % LANES

        def give(k, _, c=c, skip=skip, turn=turn):
            b = peer(me, k)
            for h in range(2):
                a = (2 * b + h - skip) & (2 * n - 1)
                z = (2 * b + h - skip - 1) & (2 * n - 1)
                for p in range(per):
                    for f in range(FIELDS):
                        late = pltpu.roll(whole[c][a // 2, p, a % 2, f], turn, 1)
                        soon = pltpu.roll(whole[c][z // 2, p, z % 2, f], turn, 1)
                        value = jnp.where(lane >= turn, late, soon)
                        turned[b, f, pl.ds((c * per + p) * SUB, SUB), h * LANES : (h + 1) * LANES] = value

            src, dst = second_leg(c, b)

            @pl.when(b != me)
            def _():
                remote(src, dst, s2, r2, az=b).start()

            @pl.when(b == me)
            def _():
                pltpu.make_async_copy(src, dst, own2).start()

            return 0

        lax.fori_loop(0, n, give, 0)

    for c in range(chunks):
        wait_bytes(send.at[pl.ds(0, n - 1), pl.ds(c * per, per)], s1.at[c])
    wait_bytes(landed.at[pl.ds(0, n - 1)], s2)
    wait_bytes(landed.at[me], own2)
    wait_bytes(landed.at[pl.ds(0, n - 1)], r2)

    radial_sent()


def deliver(landed, den_o, mom_o, en_o, sems):
    rows = den_o.shape[0]
    parts = sems.shape[0]
    copies = []
    for p in range(parts):
        at = pl.ds(p * (rows // parts), rows // parts)
        copies.append(pltpu.make_async_copy(landed.at[at, 0], den_o.at[at], sems.at[p, 0]))
        for f in range(3):
            copies.append(pltpu.make_async_copy(landed.at[at, 1 + f], mom_o.at[f, at], sems.at[p, 1 + f]))
        copies.append(pltpu.make_async_copy(landed.at[at, 4], en_o.at[at], sems.at[p, 4]))
    for c in copies:
        c.start()
    for c in copies:
        c.wait()


def per_device(density, momenta, energy, shifts):
    rows, thetas, width = density.shape
    n = lax.axis_size("az")
    tiles = thetas // SUB
    chunks, early = 8, 6
    per = tiles // chunks
    half = lax.axis_size("rad") // 2
    dma = pltpu.SemaphoreType.DMA
    f32 = jnp.float32
    hbm = pl.BlockSpec(memory_space=pltpu.HBM)
    landed = pl.pallas_call(
        functools.partial(kernel, chunks, early),
        out_shape=pltpu.VMEM((n, FIELDS, thetas, width), f32),
        in_specs=[hbm] * 4,
        out_specs=pl.BlockSpec(memory_space=pltpu.VMEM),
        scratch_shapes=[
            pltpu.SMEM((rows,), jnp.int32),
            pltpu.VMEM((FIELDS, rows + 2, thetas, width), f32),
            pltpu.VMEM((rows, tiles, 2, FIELDS, SUB, LANES), f32),
            pltpu.VMEM((n, FIELDS, thetas, width), f32),
            pltpu.VMEM((2, tiles, SUB, LANES), f32),
            pltpu.VMEM((2, tiles, SUB, LANES), f32),
            pltpu.VMEM((2, half, FIELDS, thetas // half, width), f32),
            *[pltpu.VMEM((n, per, 2, FIELDS, SUB, LANES), f32) for _ in range(chunks)],
            dma((2, 3)),
            dma,
            dma((2, 3)),
            dma((2, 3)),
            dma((2, half)),
            dma((2, half)),
            dma((2, 2)),
            dma((2, 2)),
            dma((chunks,)),
            dma((chunks,)),
            dma((chunks,)),
            dma,
            dma,
            dma,
        ],
        compiler_params=pltpu.CompilerParams(
            collective_id=0, has_side_effects=True, vmem_limit_bytes=56 * 2**20
        ),
        name="transport",
    )(density, momenta, energy, shifts)
    return pl.pallas_call(
        deliver,
        out_shape=[jax.ShapeDtypeStruct(x.shape, f32) for x in (density, momenta, energy)],
        in_specs=[pl.BlockSpec(memory_space=pl.ANY)],
        out_specs=[pl.BlockSpec(memory_space=pl.ANY)] * 3,
        scratch_shapes=[dma((4, FIELDS))],
        compiler_params=pltpu.CompilerParams(vmem_limit_bytes=2**20),
        name="deliver",
    )(landed)


def solution(mesh):
    return jax.shard_map(
        per_device,
        mesh=mesh,
        in_specs=(P("rad", None, "az"), P(None, "rad", None, "az"), P("rad", None, "az"), P("rad")),
        out_specs=(P("rad", None, "az"), P(None, "rad", None, "az"), P("rad", None, "az")),
        check_vma=False,
    )
```

```python
import functools

import jax
import jax.numpy as jnp
from jax import lax
from jax.experimental import pallas as pl
from jax.experimental.pallas import tpu as pltpu
from jax.sharding import PartitionSpec as P

MESH = pl.DeviceIdType.MESH
LANES = 128
SUB = 8
FIELDS = 5


def remote(src, dst, send, recv, **where):
    return pltpu.make_async_remote_copy(
        src_ref=src, dst_ref=dst, send_sem=send, recv_sem=recv, device_id=where, device_id_type=MESH
    )


def wait_bytes(ref, sem):
    pltpu.make_async_copy(ref, ref, sem).wait()


def peer(me, k):
    y = (me // 4 + k) % 4
    x = (me // 2 + k // 4) % 2
    core = (me + k // 8) % 2
    return y * 4 + x * 2 + core


def kernel(chunks, early, den, mom, en, shifts, landed, *refs):
    amounts, st, send, turned, pack, halo, relay = refs[:7]
    whole = refs[7 : 7 + chunks]
    in_sem, shift_sem, rad_send, rad_recv, relay_send, relay_recv, az_send, az_recv, s1, r1, own1, s2, r2, own2 = refs[7 + chunks :]
    rows = den.shape[0]
    tiles = den.shape[1] // SUB
    per = tiles // chunks
    me = lax.axis_index("az")
    n = lax.axis_size("az")
    pos = lax.axis_index("rad")
    groups = lax.axis_size("rad")
    at_inner = pos == 0
    at_outer = pos == groups - 1

    def load(j, first, count):
        at = pl.ds(first * SUB, count * SUB)
        return [
            pltpu.make_async_copy(den.at[:, at], st.at[0, pl.ds(1, rows), at], in_sem.at[j, 0]),
            pltpu.make_async_copy(mom.at[:, :, at], st.at[pl.ds(1, 3), pl.ds(1, rows), at], in_sem.at[j, 1]),
            pltpu.make_async_copy(en.at[:, at], st.at[4, pl.ds(1, rows), at], in_sem.at[j, 2]),
        ]

    loads = [load(0, 0, 2), load(1, 2, tiles - 2)]
    get_shifts = pltpu.make_async_copy(shifts, amounts, shift_sem)
    for part in loads:
        for c in part:
            c.start()
    get_shifts.start()

    barrier = pltpu.get_barrier_semaphore()

    def greet(k, _):
        pl.semaphore_signal(barrier, 1, device_id={"az": peer(me, k)}, device_id_type=MESH)
        return 0

    lax.fori_loop(1, n, greet, 0)

    half = groups // 2
    across = (pos + half) % groups
    has_out = jnp.logical_not(at_outer) & (pos != half - 1)
    has_in = jnp.logical_not(at_inner) & (pos != half)
    pl.semaphore_signal(barrier, 1, device_id={"rad": across}, device_id_type=MESH)

    @pl.when(has_out)
    def _():
        pl.semaphore_signal(barrier, 1, device_id={"rad": pos + 1}, device_id_type=MESH)

    @pl.when(has_in)
    def _():
        pl.semaphore_signal(barrier, 1, device_id={"rad": pos - 1}, device_id_type=MESH)

    lane = lax.broadcasted_iota(jnp.int32, (SUB, LANES), 1)
    sub = lax.broadcasted_iota(jnp.int32, (SUB, LANES), 0)

    def packing(t, _):
        at = pl.ds(pl.multiple_of(t * SUB, SUB), SUB)
        first = jnp.zeros((SUB, LANES), jnp.float32)
        last = jnp.zeros((SUB, LANES), jnp.float32)
        for f in range(FIELDS):
            for i in range(rows):
                k = f * rows + i
                low = st[f, 1 + i, at, 0:LANES]
                high = st[f, 1 + i, at, LANES : 2 * LANES]
                first = jnp.where(lane == k, pltpu.roll(low, k, 1) if k else low, first)
                last = jnp.where(lane == k, pltpu.roll(high, k + 1, 1), last)
        pack[0, t] = first
        pack[1, t] = last
        return 0

    def edges(j, first, count):
        at = pl.ds(first, count)
        return [
            remote(pack.at[1, at], halo.at[0, at], az_send.at[j, 0], az_recv.at[j, 0], az=(me + 1) % n),
            remote(pack.at[0, at], halo.at[1, at], az_send.at[j, 1], az_recv.at[j, 1], az=(me + n - 1) % n),
        ]

    azimuthal = [edges(0, 0, 1), edges(1, 1, tiles - 1)]
    for c in loads[0]:
        c.wait()
    packing(0, 0)
    pl.semaphore_wait(barrier, n + jnp.where(has_out, 1, 0) + jnp.where(has_in, 1, 0))
    for c in azimuthal[0]:
        c.start()

    def radial(way, row, slot, to):
        srcs = [den.at[row], mom.at[:, row], en.at[row]]
        dsts = [st.at[0, slot], st.at[pl.ds(1, 3), slot], st.at[4, slot]]
        return [remote(a, b, rad_send.at[way, j], rad_recv.at[way, j], rad=to) for j, (a, b) in enumerate(zip(srcs, dsts))]

    outward = radial(0, rows - 1, 0, (pos + 1) % groups)
    inward = radial(1, 0, rows + 1, (pos + groups - 1) % groups)

    part_rows = tiles * SUB // half
    low = pos < half
    place = pos % half

    def seam_part(way, p):
        carries = jnp.where(low, p <= place, p >= place)
        crossing = low if way == 0 else jnp.logical_not(low)
        step = groups - 1 if way == 0 else 1
        to = jnp.where(crossing & (p == place), across, (pos + step) % groups)
        last = pos == (half if way == 0 else half - 1)
        at = pl.ds(p * part_rows, part_rows)
        row = rows - 1 if way == 0 else 0
        edge = [den.at[row, at], mom.at[:, row, at], en.at[row, at]]
        slot = [relay.at[way, p, 0], relay.at[way, p, pl.ds(1, 3)], relay.at[way, p, 4]]

        def copy(src, dst):
            return remote(src, dst, relay_send.at[way, p], relay_recv.at[way, p], rad=to)

        first = [copy(a, b) for a, b in zip(edge, slot)]
        return carries, carries & jnp.logical_not(last), copy(relay.at[way, p], relay.at[way, p]), first

    def seam(stage):
        for way in range(2):
            hops = jnp.where(low, half - 1 - place, half - place) if way == 0 else jnp.where(low, place + 1, place)

            @pl.when(hops == stage)
            def _():
                for p in range(half):
                    carries, hands_on, onward, first = seam_part(way, p)
                    if stage == 0:
                        @pl.when(carries)
                        def _():
                            for a in first:
                                a.start()
                    else:
                        @pl.when(carries)
                        def _():
                            onward.wait_recv()

                        @pl.when(hands_on)
                        def _():
                            onward.start()

    seam(0)

    @pl.when(has_out)
    def _():
        for c in outward:
            c.start()

    @pl.when(has_in)
    def _():
        for c in inward:
            c.start()

    def seam_into_state():
        for way in range(2):
            @pl.when(pos == (half if way == 0 else half - 1))
            def _():
                for p in range(half):
                    st[:, 0 if way == 0 else rows + 1, p * part_rows : (p + 1) * part_rows] = relay[way, p]

    def radial_arrived():
        @pl.when(has_in)
        def _():
            for c in outward:
                c.wait_recv()

        @pl.when(has_out)
        def _():
            for c in inward:
                c.wait_recv()

        @pl.when(at_inner)
        def _():
            st[:, 0] = st[:, 1]

        @pl.when(at_outer)
        def _():
            st[:, rows + 1] = st[:, rows]

    def radial_sent():
        @pl.when(has_out)
        def _():
            for c in outward:
                c.wait_send()

        @pl.when(has_in)
        def _():
            for c in inward:
                c.wait_send()

        for way in range(2):
            for p in range(half):
                carries, hands_on, onward, first = seam_part(way, p)

                @pl.when(hands_on)
                def _():
                    onward.wait_send()

    for c in loads[1]:
        c.wait()
    lax.fori_loop(1, tiles, packing, 0)
    for c in azimuthal[1]:
        c.start()
    get_shifts.wait()

    total = groups * rows

    def radius(index):
        return 1.0 + 2.0 * (index.astype(jnp.float32) + 0.5) / total

    def upwind(face, low, high):
        return face * jnp.where(face > 0, low, high)

    def compute(row, t):
        t0 = pl.multiple_of(t * SUB, SUB)
        at = pl.ds(t0, SUB)
        at_dn = pl.ds(pl.multiple_of(jnp.maximum(t - 1, 0) * SUB, SUB), SUB)
        at_up = pl.ds(pl.multiple_of(jnp.minimum(t + 1, tiles - 1) * SUB, SUB), SUB)
        index = pos * rows + row
        here = radius(index)
        face_up = 0.5 * (here + radius(index + 1))
        face_dn = 0.5 * (radius(index - 1) + here)
        area = jnp.full((SUB, LANES), here * here, jnp.float32)
        w_up = jnp.full((SUB, LANES), face_up * face_up, jnp.float32) / area
        w_dn = jnp.full((SUB, LANES), face_dn * face_dn, jnp.float32) / area
        w_up = jnp.where(index == total - 1, 0.0, w_up)
        w_dn = jnp.where(index == 0, 0.0, w_dn)
        before = halo[0, t]
        after = halo[1, t]
        q = [[st[f, row + 1, at, h * LANES : (h + 1) * LANES] for h in range(2)] for f in range(FIELDS)]
        back, ahead = [], []
        for f in range(FIELDS):
            k = f * rows + row
            b = pltpu.roll(before, (LANES - k) % LANES, 1)
            a = pltpu.roll(after, LANES - 1 - k, 1)
            low, high = q[f]
            low_r, high_r = pltpu.roll(low, 1, 1), pltpu.roll(high, 1, 1)
            low_l, high_l = pltpu.roll(low, LANES - 1, 1), pltpu.roll(high, LANES - 1, 1)
            back.append([jnp.where(lane == 0, b, low_r), jnp.where(lane == 0, low_r, high_r)])
            ahead.append(
                [jnp.where(lane == LANES - 1, high_l, low_l), jnp.where(lane == LANES - 1, a, high_l)]
            )
        for h in range(2):
            cols = slice(h * LANES, (h + 1) * LANES)
            c = [q[f][h] for f in range(FIELDS)]
            inner = [st[f, row, at, cols] for f in range(FIELDS)]
            outer = [st[f, row + 2, at, cols] for f in range(FIELDS)]
            above, below = [], []
            for f in range(FIELDS):
                prev = st[f, row + 1, at_dn, cols]
                nxt = st[f, row + 1, at_up, cols]
                below.append(pltpu.roll(jnp.where(sub == SUB - 1, prev, c[f]), 1, 0))
                above.append(pltpu.roll(jnp.where(sub == 0, nxt, c[f]), SUB - 1, 0))
            below[4] = jnp.where(t0 + sub == 0, c[4], below[4])
            above[4] = jnp.where(t0 + sub == tiles * SUB - 1, c[4], above[4])
            inv = 1.0 / c[0]
            v_r, v_p, v_t = c[1] * inv, c[2] * inv, c[3] * inv
            r_up = 0.5 * (v_r + outer[1] / outer[0])
            r_dn = 0.5 * (v_r + inner[1] / inner[0])
            p_up = 0.5 * (v_p + ahead[2][h] / ahead[0][h])
            p_dn = 0.5 * (v_p + back[2][h] / back[0][h])
            t_up_v = jnp.where(t0 + sub == tiles * SUB - 1, 0.0, 0.5 * (v_t + above[3] / above[0]))
            t_dn_v = jnp.where(t0 + sub == 0, 0.0, 0.5 * (v_t + below[3] / below[0]))
            r_up_w, r_dn_w = r_up * w_up, r_dn * w_dn
            for f in range(FIELDS):
                out = c[f]
                out -= r_up_w * jnp.where(r_up > 0, c[f], outer[f]) - r_dn_w * jnp.where(r_dn > 0, inner[f], c[f])
                out -= upwind(t_up_v, c[f], above[f]) - upwind(t_dn_v, below[f], c[f])
                out -= upwind(p_up, c[f], ahead[f][h]) - upwind(p_dn, back[f][h], c[f])
                if f == 1:
                    out -= 0.5 * (0.5 * (0.4 * outer[4] - 0.4 * inner[4]))
                if f == 2:
                    out -= 0.5 * (0.5 * (0.4 * ahead[4][h] - 0.4 * back[4][h]))
                if f == 3:
                    out -= 0.5 * (0.5 * (0.4 * above[4] - 0.4 * below[4]))
                send[row, t, h, f] = out

    def whole_row(row, c):
        lax.fori_loop(0, per, lambda p, _: (compute(row, c * per + p), 0)[1], 0)

    def turn_of(c):
        return (c % 2 * 4 + c // 2 % 2 * 2 + c // 4) * (rows // 8) % rows

    def first_leg(c, row):
        part = send.at[row, pl.ds(c * per, per)]
        return part, whole[c].at[me]

    def produce(c, wanted):
        def step(k, _):
            to = peer(me, k)
            row = (to + n - turn_of(c)) % n

            def do():
                whole_row(row, c)
                part, place = first_leg(c, row)

                @pl.when(to != me)
                def _():
                    remote(part, place, s1.at[c], r1.at[c], az=to).start()

                @pl.when(to == me)
                def _():
                    pltpu.make_async_copy(part, place, own1.at[c]).start()

            edge = (row == 0) | (row == rows - 1)
            if wanted == "every":
                do()
            elif wanted == "edges":
                pl.when(edge)(do)
            else:
                pl.when(jnp.logical_not(edge))(do)
            return 0

        lax.fori_loop(0, rows, step, 0)

    for c in azimuthal[0]:
        c.wait()
    for c in range(chunks):
        produce(c, "inside" if c < early else "every")
        if c == 0:
            for a in azimuthal[1]:
                a.wait()
        if 1 <= c - early + half + 1 <= half:
            seam(c - early + half + 1)
        if c == early - 1:
            radial_arrived()
            seam_into_state()
            for e in range(early):
                produce(e, "edges")

    def second_leg(c, b):
        thetas = pl.ds(c * per * SUB, per * SUB)
        return turned.at[b, :, thetas], landed.at[(me + n - turn_of(c)) % n, :, thetas]

    for c in range(chunks):
        wait_bytes(whole[c].at[pl.ds(0, n - 1)], r1.at[c])
        pltpu.make_async_copy(send.at[me, pl.ds(c * per, per)], whole[c].at[me], own1.at[c]).wait()

        amount = amounts[(me + n - turn_of(c)) % n]
        skip = amount // LANES
        turn = amount % LANES

        def give(k, _, c=c, skip=skip, turn=turn):
            b = peer(me, k)
            for h in range(2):
                a = (2 * b + h - skip) & (2 * n - 1)
                z = (2 * b + h - skip - 1) & (2 * n - 1)
                for p in range(per):
                    for f in range(FIELDS):
                        late = pltpu.roll(whole[c][a // 2, p, a % 2, f], turn, 1)
                        soon = pltpu.roll(whole[c][z // 2, p, z % 2, f], turn, 1)
                        value = jnp.where(lane >= turn, late, soon)
                        turned[b, f, pl.ds((c * per + p) * SUB, SUB), h * LANES : (h + 1) * LANES] = value

            src, dst = second_leg(c, b)

            @pl.when(b != me)
            def _():
                remote(src, dst, s2, r2, az=b).start()

            @pl.when(b == me)
            def _():
                pltpu.make_async_copy(src, dst, own2).start()

            return 0

        lax.fori_loop(0, n, give, 0)

    for c in range(chunks):
        wait_bytes(send.at[pl.ds(0, n - 1), pl.ds(c * per, per)], s1.at[c])
    wait_bytes(landed.at[pl.ds(0, n - 1)], s2)
    wait_bytes(landed.at[me], own2)
    wait_bytes(landed.at[pl.ds(0, n - 1)], r2)

    radial_sent()


def deliver(landed, den_o, mom_o, en_o, sems):
    rows = den_o.shape[0]
    parts = sems.shape[0]
    copies = []
    for p in range(parts):
        at = pl.ds(p * (rows // parts), rows // parts)
        copies.append(pltpu.make_async_copy(landed.at[at, 0], den_o.at[at], sems.at[p, 0]))
        for f in range(3):
            copies.append(pltpu.make_async_copy(landed.at[at, 1 + f], mom_o.at[f, at], sems.at[p, 1 + f]))
        copies.append(pltpu.make_async_copy(landed.at[at, 4], en_o.at[at], sems.at[p, 4]))
    for c in copies:
        c.start()
    for c in copies:
        c.wait()


def per_device(density, momenta, energy, shifts):
    rows, thetas, width = density.shape
    n = lax.axis_size("az")
    tiles = thetas // SUB
    chunks, early = 8, 6
    per = tiles // chunks
    half = lax.axis_size("rad") // 2
    dma = pltpu.SemaphoreType.DMA
    f32 = jnp.float32
    hbm = pl.BlockSpec(memory_space=pltpu.HBM)
    landed = pl.pallas_call(
        functools.partial(kernel, chunks, early),
        out_shape=pltpu.VMEM((n, FIELDS, thetas, width), f32),
        in_specs=[hbm] * 4,
        out_specs=pl.BlockSpec(memory_space=pltpu.VMEM),
        scratch_shapes=[
            pltpu.SMEM((rows,), jnp.int32),
            pltpu.VMEM((FIELDS, rows + 2, thetas, width), f32),
            pltpu.VMEM((rows, tiles, 2, FIELDS, SUB, LANES), f32),
            pltpu.VMEM((n, FIELDS, thetas, width), f32),
            pltpu.VMEM((2, tiles, SUB, LANES), f32),
            pltpu.VMEM((2, tiles, SUB, LANES), f32),
            pltpu.VMEM((2, half, FIELDS, thetas // half, width), f32),
            *[pltpu.VMEM((n, per, 2, FIELDS, SUB, LANES), f32) for _ in range(chunks)],
            dma((2, 3)),
            dma,
            dma((2, 3)),
            dma((2, 3)),
            dma((2, half)),
            dma((2, half)),
            dma((2, 2)),
            dma((2, 2)),
            dma((chunks,)),
            dma((chunks,)),
            dma((chunks,)),
            dma,
            dma,
            dma,
        ],
        compiler_params=pltpu.CompilerParams(
            collective_id=0, has_side_effects=True, vmem_limit_bytes=56 * 2**20
        ),
        name="transport",
    )(density, momenta, energy, shifts)
    return pl.pallas_call(
        deliver,
        out_shape=[jax.ShapeDtypeStruct(x.shape, f32) for x in (density, momenta, energy)],
        in_specs=[pl.BlockSpec(memory_space=pl.ANY)],
        out_specs=[pl.BlockSpec(memory_space=pl.ANY)] * 3,
        scratch_shapes=[dma((4, FIELDS))],
        compiler_params=pltpu.CompilerParams(vmem_limit_bytes=2**20),
        name="deliver",
    )(landed)


def solution(mesh):
    return jax.shard_map(
        per_device,
        mesh=mesh,
        in_specs=(P("rad", None, "az"), P(None, "rad", None, "az"), P("rad", None, "az"), P("rad")),
        out_specs=(P("rad", None, "az"), P(None, "rad", None, "az"), P("rad", None, "az")),
        check_vma=False,
    )
```

```python
import functools

import jax
import jax.numpy as jnp
from jax import lax
from jax.experimental import pallas as pl
from jax.experimental.pallas import tpu as pltpu
from jax.sharding import PartitionSpec as P

MESH = pl.DeviceIdType.MESH
LANES = 128
SUB = 8
FIELDS = 5


def remote(src, dst, send, recv, **where):
    return pltpu.make_async_remote_copy(
        src_ref=src, dst_ref=dst, send_sem=send, recv_sem=recv, device_id=where, device_id_type=MESH
    )


def wait_bytes(ref, sem):
    pltpu.make_async_copy(ref, ref, sem).wait()


def peer(me, k):
    y = (me // 4 + k) % 4
    x = (me // 2 + k // 4) % 2
    core = (me + k // 8) % 2
    return y * 4 + x * 2 + core


def kernel(chunks, early, den, mom, en, shifts, landed, *refs):
    amounts, st, send, turned, pack, halo, relay = refs[:7]
    whole = refs[7 : 7 + chunks]
    in_sem, shift_sem, rad_send, rad_recv, relay_send, relay_recv, az_send, az_recv, s1, r1, own1, s2, r2, own2 = refs[7 + chunks :]
    rows = den.shape[0]
    tiles = den.shape[1] // SUB
    per = tiles // chunks
    me = lax.axis_index("az")
    n = lax.axis_size("az")
    pos = lax.axis_index("rad")
    groups = lax.axis_size("rad")
    at_inner = pos == 0
    at_outer = pos == groups - 1

    def load(j, first, count):
        at = pl.ds(first * SUB, count * SUB)
        return [
            pltpu.make_async_copy(den.at[:, at], st.at[0, pl.ds(1, rows), at], in_sem.at[j, 0]),
            pltpu.make_async_copy(mom.at[:, :, at], st.at[pl.ds(1, 3), pl.ds(1, rows), at], in_sem.at[j, 1]),
            pltpu.make_async_copy(en.at[:, at], st.at[4, pl.ds(1, rows), at], in_sem.at[j, 2]),
        ]

    loads = [load(0, 0, 1), load(1, 1, tiles - 1)]
    get_shifts = pltpu.make_async_copy(shifts, amounts, shift_sem)
    for part in loads:
        for c in part:
            c.start()
    get_shifts.start()

    barrier = pltpu.get_barrier_semaphore()

    def greet(k, _):
        pl.semaphore_signal(barrier, 1, device_id={"az": peer(me, k)}, device_id_type=MESH)
        return 0

    lax.fori_loop(1, n, greet, 0)

    half = groups // 2
    across = (pos + half) % groups
    has_out = jnp.logical_not(at_outer) & (pos != half - 1)
    has_in = jnp.logical_not(at_inner) & (pos != half)
    pl.semaphore_signal(barrier, 1, device_id={"rad": across}, device_id_type=MESH)

    @pl.when(has_out)
    def _():
        pl.semaphore_signal(barrier, 1, device_id={"rad": pos + 1}, device_id_type=MESH)

    @pl.when(has_in)
    def _():
        pl.semaphore_signal(barrier, 1, device_id={"rad": pos - 1}, device_id_type=MESH)

    lane = lax.broadcasted_iota(jnp.int32, (SUB, LANES), 1)
    sub = lax.broadcasted_iota(jnp.int32, (SUB, LANES), 0)

    def packing(t, _):
        at = pl.ds(pl.multiple_of(t * SUB, SUB), SUB)
        first = jnp.zeros((SUB, LANES), jnp.float32)
        last = jnp.zeros((SUB, LANES), jnp.float32)
        for f in range(FIELDS):
            for i in range(rows):
                k = f * rows + i
                low = st[f, 1 + i, at, 0:LANES]
                high = st[f, 1 + i, at, LANES : 2 * LANES]
                first = jnp.where(lane == k, pltpu.roll(low, k, 1) if k else low, first)
                last = jnp.where(lane == k, pltpu.roll(high, k + 1, 1), last)
        pack[0, t] = first
        pack[1, t] = last
        return 0

    def edges(j, first, count):
        at = pl.ds(first, count)
        return [
            remote(pack.at[1, at], halo.at[0, at], az_send.at[j, 0], az_recv.at[j, 0], az=(me + 1) % n),
            remote(pack.at[0, at], halo.at[1, at], az_send.at[j, 1], az_recv.at[j, 1], az=(me + n - 1) % n),
        ]

    azimuthal = [edges(0, 0, 1), edges(1, 1, tiles - 1)]
    for c in loads[0]:
        c.wait()
    packing(0, 0)
    pl.semaphore_wait(barrier, n + jnp.where(has_out, 1, 0) + jnp.where(has_in, 1, 0))
    for c in azimuthal[0]:
        c.start()

    def radial(way, row, slot, to):
        srcs = [den.at[row], mom.at[:, row], en.at[row]]
        dsts = [st.at[0, slot], st.at[pl.ds(1, 3), slot], st.at[4, slot]]
        return [remote(a, b, rad_send.at[way, j], rad_recv.at[way, j], rad=to) for j, (a, b) in enumerate(zip(srcs, dsts))]

    outward = radial(0, rows - 1, 0, (pos + 1) % groups)
    inward = radial(1, 0, rows + 1, (pos + groups - 1) % groups)

    part_rows = tiles * SUB // half
    low = pos < half
    place = pos % half

    def seam_part(way, p):
        carries = jnp.where(low, p <= place, p >= place)
        crossing = low if way == 0 else jnp.logical_not(low)
        step = groups - 1 if way == 0 else 1
        to = jnp.where(crossing & (p == place), across, (pos + step) % groups)
        last = pos == (half if way == 0 else half - 1)
        at = pl.ds(p * part_rows, part_rows)
        row = rows - 1 if way == 0 else 0
        edge = [den.at[row, at], mom.at[:, row, at], en.at[row, at]]
        slot = [relay.at[way, p, 0], relay.at[way, p, pl.ds(1, 3)], relay.at[way, p, 4]]

        def copy(src, dst):
            return remote(src, dst, relay_send.at[way, p], relay_recv.at[way, p], rad=to)

        first = [copy(a, b) for a, b in zip(edge, slot)]
        return carries, carries & jnp.logical_not(last), copy(relay.at[way, p], relay.at[way, p]), first

    def seam(stage):
        for way in range(2):
            hops = jnp.where(low, half - 1 - place, half - place) if way == 0 else jnp.where(low, place + 1, place)

            @pl.when(hops == stage)
            def _():
                for p in range(half):
                    carries, hands_on, onward, first = seam_part(way, p)
                    if stage == 0:
                        @pl.when(carries)
                        def _():
                            for a in first:
                                a.start()
                    else:
                        @pl.when(carries)
                        def _():
                            onward.wait_recv()

                        @pl.when(hands_on)
                        def _():
                            onward.start()

    seam(0)

    @pl.when(has_out)
    def _():
        for c in outward:
            c.start()

    @pl.when(has_in)
    def _():
        for c in inward:
            c.start()

    def seam_into_state():
        for way in range(2):
            @pl.when(pos == (half if way == 0 else half - 1))
            def _():
                for p in range(half):
                    st[:, 0 if way == 0 else rows + 1, p * part_rows : (p + 1) * part_rows] = relay[way, p]

    def radial_arrived():
        @pl.when(has_in)
        def _():
            for c in outward:
                c.wait_recv()

        @pl.when(has_out)
        def _():
            for c in inward:
                c.wait_recv()

        @pl.when(at_inner)
        def _():
            st[:, 0] = st[:, 1]

        @pl.when(at_outer)
        def _():
            st[:, rows + 1] = st[:, rows]

    def radial_sent():
        @pl.when(has_out)
        def _():
            for c in outward:
                c.wait_send()

        @pl.when(has_in)
        def _():
            for c in inward:
                c.wait_send()

        for way in range(2):
            for p in range(half):
                carries, hands_on, onward, first = seam_part(way, p)

                @pl.when(hands_on)
                def _():
                    onward.wait_send()

    for c in loads[1]:
        c.wait()
    lax.fori_loop(1, tiles, packing, 0)
    for c in azimuthal[1]:
        c.start()
    get_shifts.wait()

    total = groups * rows

    def radius(index):
        return 1.0 + 2.0 * (index.astype(jnp.float32) + 0.5) / total

    def upwind(face, low, high):
        return face * jnp.where(face > 0, low, high)

    def compute(row, t):
        t0 = pl.multiple_of(t * SUB, SUB)
        at = pl.ds(t0, SUB)
        at_dn = pl.ds(pl.multiple_of(jnp.maximum(t - 1, 0) * SUB, SUB), SUB)
        at_up = pl.ds(pl.multiple_of(jnp.minimum(t + 1, tiles - 1) * SUB, SUB), SUB)
        index = pos * rows + row
        here = radius(index)
        face_up = 0.5 * (here + radius(index + 1))
        face_dn = 0.5 * (radius(index - 1) + here)
        area = jnp.full((SUB, LANES), here * here, jnp.float32)
        w_up = jnp.full((SUB, LANES), face_up * face_up, jnp.float32) / area
        w_dn = jnp.full((SUB, LANES), face_dn * face_dn, jnp.float32) / area
        w_up = jnp.where(index == total - 1, 0.0, w_up)
        w_dn = jnp.where(index == 0, 0.0, w_dn)
        before = halo[0, t]
        after = halo[1, t]
        q = [[st[f, row + 1, at, h * LANES : (h + 1) * LANES] for h in range(2)] for f in range(FIELDS)]
        back, ahead = [], []
        for f in range(FIELDS):
            k = f * rows + row
            b = pltpu.roll(before, (LANES - k) % LANES, 1)
            a = pltpu.roll(after, LANES - 1 - k, 1)
            low, high = q[f]
            low_r, high_r = pltpu.roll(low, 1, 1), pltpu.roll(high, 1, 1)
            low_l, high_l = pltpu.roll(low, LANES - 1, 1), pltpu.roll(high, LANES - 1, 1)
            back.append([jnp.where(lane == 0, b, low_r), jnp.where(lane == 0, low_r, high_r)])
            ahead.append(
                [jnp.where(lane == LANES - 1, high_l, low_l), jnp.where(lane == LANES - 1, a, high_l)]
            )
        for h in range(2):
            cols = slice(h * LANES, (h + 1) * LANES)
            c = [q[f][h] for f in range(FIELDS)]
            inner = [st[f, row, at, cols] for f in range(FIELDS)]
            outer = [st[f, row + 2, at, cols] for f in range(FIELDS)]
            above, below = [], []
            for f in range(FIELDS):
                prev = st[f, row + 1, at_dn, cols]
                nxt = st[f, row + 1, at_up, cols]
                below.append(pltpu.roll(jnp.where(sub == SUB - 1, prev, c[f]), 1, 0))
                above.append(pltpu.roll(jnp.where(sub == 0, nxt, c[f]), SUB - 1, 0))
            below[4] = jnp.where(t0 + sub == 0, c[4], below[4])
            above[4] = jnp.where(t0 + sub == tiles * SUB - 1, c[4], above[4])
            inv = 1.0 / c[0]
            v_r, v_p, v_t = c[1] * inv, c[2] * inv, c[3] * inv
            r_up = 0.5 * (v_r + outer[1] / outer[0])
            r_dn = 0.5 * (v_r + inner[1] / inner[0])
            p_up = 0.5 * (v_p + ahead[2][h] / ahead[0][h])
            p_dn = 0.5 * (v_p + back[2][h] / back[0][h])
            t_up_v = jnp.where(t0 + sub == tiles * SUB - 1, 0.0, 0.5 * (v_t + above[3] / above[0]))
            t_dn_v = jnp.where(t0 + sub == 0, 0.0, 0.5 * (v_t + below[3] / below[0]))
            r_up_w, r_dn_w = r_up * w_up, r_dn * w_dn
            for f in range(FIELDS):
                out = c[f]
                out -= r_up_w * jnp.where(r_up > 0, c[f], outer[f]) - r_dn_w * jnp.where(r_dn > 0, inner[f], c[f])
                out -= upwind(t_up_v, c[f], above[f]) - upwind(t_dn_v, below[f], c[f])
                out -= upwind(p_up, c[f], ahead[f][h]) - upwind(p_dn, back[f][h], c[f])
                if f == 1:
                    out -= 0.5 * (0.5 * (0.4 * outer[4] - 0.4 * inner[4]))
                if f == 2:
                    out -= 0.5 * (0.5 * (0.4 * ahead[4][h] - 0.4 * back[4][h]))
                if f == 3:
                    out -= 0.5 * (0.5 * (0.4 * above[4] - 0.4 * below[4]))
                send[row, t, h, f] = out

    def whole_row(row, c):
        lax.fori_loop(0, per, lambda p, _: (compute(row, c * per + p), 0)[1], 0)

    def turn_of(c):
        return (c % 2 * 4 + c // 2 % 2 * 2 + c // 4) * (rows // 8) % rows

    def first_leg(c, row):
        part = send.at[row, pl.ds(c * per, per)]
        return part, whole[c].at[me]

    def produce(c, wanted):
        def step(k, _):
            to = peer(me, k)
            row = (to + n - turn_of(c)) % n

            def do():
                whole_row(row, c)
                part, place = first_leg(c, row)

                @pl.when(to != me)
                def _():
                    remote(part, place, s1.at[c], r1.at[c], az=to).start()

                @pl.when(to == me)
                def _():
                    pltpu.make_async_copy(part, place, own1.at[c]).start()

            edge = (row == 0) | (row == rows - 1)
            if wanted == "every":
                do()
            elif wanted == "edges":
                pl.when(edge)(do)
            else:
                pl.when(jnp.logical_not(edge))(do)
            return 0

        lax.fori_loop(1, n + 1, step, 0)

    for c in azimuthal[0]:
        c.wait()
    for c in range(chunks):
        produce(c, "inside" if c < early else "every")
        if c == 0:
            for a in azimuthal[1]:
                a.wait()
        if 1 <= c - early + half + 1 <= half:
            seam(c - early + half + 1)
        if c == early - 1:
            radial_arrived()
            seam_into_state()
            for e in range(early):
                produce(e, "edges")

    def second_leg(c, b):
        thetas = pl.ds(c * per * SUB, per * SUB)
        return turned.at[b, :, thetas], landed.at[(me + n - turn_of(c)) % n, :, thetas]

    for c in range(chunks):
        wait_bytes(whole[c].at[pl.ds(0, n - 1)], r1.at[c])
        pltpu.make_async_copy(send.at[me, pl.ds(c * per, per)], whole[c].at[me], own1.at[c]).wait()

        amount = amounts[(me + n - turn_of(c)) % n]
        skip = amount // LANES
        turn = amount % LANES

        def give(k, _, c=c, skip=skip, turn=turn):
            b = peer(me, k)
            for h in range(2):
                a = (2 * b + h - skip) & (2 * n - 1)
                z = (2 * b + h - skip - 1) & (2 * n - 1)
                for p in range(per):
                    for f in range(FIELDS):
                        late = pltpu.roll(whole[c][a // 2, p, a % 2, f], turn, 1)
                        soon = pltpu.roll(whole[c][z // 2, p, z % 2, f], turn, 1)
                        value = jnp.where(lane >= turn, late, soon)
                        turned[b, f, pl.ds((c * per + p) * SUB, SUB), h * LANES : (h + 1) * LANES] = value

            src, dst = second_leg(c, b)

            @pl.when(b != me)
            def _():
                remote(src, dst, s2, r2, az=b).start()

            @pl.when(b == me)
            def _():
                pltpu.make_async_copy(src, dst, own2).start()

            return 0

        lax.fori_loop(1, n + 1, give, 0)

    for c in range(chunks):
        wait_bytes(send.at[pl.ds(0, n - 1), pl.ds(c * per, per)], s1.at[c])
    wait_bytes(landed.at[pl.ds(0, n - 1)], s2)
    wait_bytes(landed.at[me], own2)
    wait_bytes(landed.at[pl.ds(0, n - 1)], r2)

    radial_sent()


def deliver(landed, den_o, mom_o, en_o, sems):
    rows = den_o.shape[0]
    parts = sems.shape[0]
    copies = []
    for p in range(parts):
        at = pl.ds(p * (rows // parts), rows // parts)
        copies.append(pltpu.make_async_copy(landed.at[at, 0], den_o.at[at], sems.at[p, 0]))
        for f in range(3):
            copies.append(pltpu.make_async_copy(landed.at[at, 1 + f], mom_o.at[f, at], sems.at[p, 1 + f]))
        copies.append(pltpu.make_async_copy(landed.at[at, 4], en_o.at[at], sems.at[p, 4]))
    for c in copies:
        c.start()
    for c in copies:
        c.wait()


def per_device(density, momenta, energy, shifts):
    rows, thetas, width = density.shape
    n = lax.axis_size("az")
    tiles = thetas // SUB
    chunks, early = 8, 6
    per = tiles // chunks
    half = lax.axis_size("rad") // 2
    dma = pltpu.SemaphoreType.DMA
    f32 = jnp.float32
    hbm = pl.BlockSpec(memory_space=pltpu.HBM)
    landed = pl.pallas_call(
        functools.partial(kernel, chunks, early),
        out_shape=pltpu.VMEM((n, FIELDS, thetas, width), f32),
        in_specs=[hbm] * 4,
        out_specs=pl.BlockSpec(memory_space=pltpu.VMEM),
        scratch_shapes=[
            pltpu.SMEM((rows,), jnp.int32),
            pltpu.VMEM((FIELDS, rows + 2, thetas, width), f32),
            pltpu.VMEM((rows, tiles, 2, FIELDS, SUB, LANES), f32),
            pltpu.VMEM((n, FIELDS, thetas, width), f32),
            pltpu.VMEM((2, tiles, SUB, LANES), f32),
            pltpu.VMEM((2, tiles, SUB, LANES), f32),
            pltpu.VMEM((2, half, FIELDS, thetas // half, width), f32),
            *[pltpu.VMEM((n, per, 2, FIELDS, SUB, LANES), f32) for _ in range(chunks)],
            dma((2, 3)),
            dma,
            dma((2, 3)),
            dma((2, 3)),
            dma((2, half)),
            dma((2, half)),
            dma((2, 2)),
            dma((2, 2)),
            dma((chunks,)),
            dma((chunks,)),
            dma((chunks,)),
            dma,
            dma,
            dma,
        ],
        compiler_params=pltpu.CompilerParams(
            collective_id=0, has_side_effects=True, vmem_limit_bytes=56 * 2**20
        ),
        name="transport",
    )(density, momenta, energy, shifts)
    return pl.pallas_call(
        deliver,
        out_shape=[jax.ShapeDtypeStruct(x.shape, f32) for x in (density, momenta, energy)],
        in_specs=[pl.BlockSpec(memory_space=pl.ANY)],
        out_specs=[pl.BlockSpec(memory_space=pl.ANY)] * 3,
        scratch_shapes=[dma((1, FIELDS))],
        compiler_params=pltpu.CompilerParams(vmem_limit_bytes=2**20),
        name="deliver",
    )(landed)


def solution(mesh):
    return jax.shard_map(
        per_device,
        mesh=mesh,
        in_specs=(P("rad", None, "az"), P(None, "rad", None, "az"), P("rad", None, "az"), P("rad")),
        out_specs=(P("rad", None, "az"), P(None, "rad", None, "az"), P("rad", None, "az")),
        check_vma=False,
    )
```

```python
import functools

import jax
import jax.numpy as jnp
from jax import lax
from jax.experimental import pallas as pl
from jax.experimental.pallas import tpu as pltpu
from jax.sharding import PartitionSpec as P

MESH = pl.DeviceIdType.MESH
LANES = 128
SUB = 8
FIELDS = 5


def remote(src, dst, send, recv, **where):
    return pltpu.make_async_remote_copy(
        src_ref=src, dst_ref=dst, send_sem=send, recv_sem=recv, device_id=where, device_id_type=MESH
    )


def wait_bytes(ref, sem):
    pltpu.make_async_copy(ref, ref, sem).wait()


def peer(me, k):
    y = (me // 4 + k * (1 + me % 2 * 2)) % 4
    x = (me // 2 + k // 4) % 2
    core = (me + k // 8) % 2
    return y * 4 + x * 2 + core


def kernel(chunks, early, den, mom, en, shifts, landed, *refs):
    amounts, st, send, turned, pack, halo, relay = refs[:7]
    whole = refs[7 : 7 + chunks]
    in_sem, shift_sem, rad_send, rad_recv, relay_send, relay_recv, az_send, az_recv, s1, r1, own1, s2, r2, own2 = refs[7 + chunks :]
    rows = den.shape[0]
    tiles = den.shape[1] // SUB
    per = tiles // chunks
    me = lax.axis_index("az")
    n = lax.axis_size("az")
    pos = lax.axis_index("rad")
    groups = lax.axis_size("rad")
    at_inner = pos == 0
    at_outer = pos == groups - 1

    def load(j, first, count):
        at = pl.ds(first * SUB, count * SUB)
        return [
            pltpu.make_async_copy(den.at[:, at], st.at[0, pl.ds(1, rows), at], in_sem.at[j, 0]),
            pltpu.make_async_copy(mom.at[:, :, at], st.at[pl.ds(1, 3), pl.ds(1, rows), at], in_sem.at[j, 1]),
            pltpu.make_async_copy(en.at[:, at], st.at[4, pl.ds(1, rows), at], in_sem.at[j, 2]),
        ]

    loads = [load(0, 0, 1), load(1, 1, tiles - 1)]
    get_shifts = pltpu.make_async_copy(shifts, amounts, shift_sem)
    for part in loads:
        for c in part:
            c.start()
    get_shifts.start()

    barrier = pltpu.get_barrier_semaphore()

    def greet(k, _):
        pl.semaphore_signal(barrier, 1, device_id={"az": peer(me, k)}, device_id_type=MESH)
        return 0

    lax.fori_loop(1, n, greet, 0)

    half = groups // 2
    across = (pos + half) % groups
    has_out = jnp.logical_not(at_outer) & (pos != half - 1)
    has_in = jnp.logical_not(at_inner) & (pos != half)
    pl.semaphore_signal(barrier, 1, device_id={"rad": across}, device_id_type=MESH)

    @pl.when(has_out)
    def _():
        pl.semaphore_signal(barrier, 1, device_id={"rad": pos + 1}, device_id_type=MESH)

    @pl.when(has_in)
    def _():
        pl.semaphore_signal(barrier, 1, device_id={"rad": pos - 1}, device_id_type=MESH)

    lane = lax.broadcasted_iota(jnp.int32, (SUB, LANES), 1)
    sub = lax.broadcasted_iota(jnp.int32, (SUB, LANES), 0)

    def packing(t, _):
        at = pl.ds(pl.multiple_of(t * SUB, SUB), SUB)
        first = jnp.zeros((SUB, LANES), jnp.float32)
        last = jnp.zeros((SUB, LANES), jnp.float32)
        for f in range(FIELDS):
            for i in range(rows):
                k = f * rows + i
                low = st[f, 1 + i, at, 0:LANES]
                high = st[f, 1 + i, at, LANES : 2 * LANES]
                first = jnp.where(lane == k, pltpu.roll(low, k, 1) if k else low, first)
                last = jnp.where(lane == k, pltpu.roll(high, k + 1, 1), last)
        pack[0, t] = first
        pack[1, t] = last
        return 0

    def edges(j, first, count):
        at = pl.ds(first, count)
        return [
            remote(pack.at[1, at], halo.at[0, at], az_send.at[j, 0], az_recv.at[j, 0], az=(me + 1) % n),
            remote(pack.at[0, at], halo.at[1, at], az_send.at[j, 1], az_recv.at[j, 1], az=(me + n - 1) % n),
        ]

    azimuthal = [edges(0, 0, 1), edges(1, 1, tiles - 1)]
    for c in loads[0]:
        c.wait()
    packing(0, 0)
    pl.semaphore_wait(barrier, n + jnp.where(has_out, 1, 0) + jnp.where(has_in, 1, 0))
    for c in azimuthal[0]:
        c.start()

    def radial(way, row, slot, to):
        srcs = [den.at[row], mom.at[:, row], en.at[row]]
        dsts = [st.at[0, slot], st.at[pl.ds(1, 3), slot], st.at[4, slot]]
        return [remote(a, b, rad_send.at[way, j], rad_recv.at[way, j], rad=to) for j, (a, b) in enumerate(zip(srcs, dsts))]

    outward = radial(0, rows - 1, 0, (pos + 1) % groups)
    inward = radial(1, 0, rows + 1, (pos + groups - 1) % groups)

    part_rows = tiles * SUB // half
    low = pos < half
    place = pos % half

    def seam_part(way, p):
        carries = jnp.where(low, p <= place, p >= place)
        crossing = low if way == 0 else jnp.logical_not(low)
        step = groups - 1 if way == 0 else 1
        to = jnp.where(crossing & (p == place), across, (pos + step) % groups)
        last = pos == (half if way == 0 else half - 1)
        at = pl.ds(p * part_rows, part_rows)
        row = rows - 1 if way == 0 else 0
        edge = [den.at[row, at], mom.at[:, row, at], en.at[row, at]]
        slot = [relay.at[way, p, 0], relay.at[way, p, pl.ds(1, 3)], relay.at[way, p, 4]]

        def copy(src, dst):
            return remote(src, dst, relay_send.at[way, p], relay_recv.at[way, p], rad=to)

        first = [copy(a, b) for a, b in zip(edge, slot)]
        return carries, carries & jnp.logical_not(last), copy(relay.at[way, p], relay.at[way, p]), first

    def seam(stage):
        for way in range(2):
            hops = jnp.where(low, half - 1 - place, half - place) if way == 0 else jnp.where(low, place + 1, place)

            @pl.when(hops == stage)
            def _():
                for p in range(half):
                    carries, hands_on, onward, first = seam_part(way, p)
                    if stage == 0:
                        @pl.when(carries)
                        def _():
                            for a in first:
                                a.start()
                    else:
                        @pl.when(carries)
                        def _():
                            onward.wait_recv()

                        @pl.when(hands_on)
                        def _():
                            onward.start()

    seam(0)

    @pl.when(has_out)
    def _():
        for c in outward:
            c.start()

    @pl.when(has_in)
    def _():
        for c in inward:
            c.start()

    def seam_into_state():
        for way in range(2):
            @pl.when(pos == (half if way == 0 else half - 1))
            def _():
                for p in range(half):
                    st[:, 0 if way == 0 else rows + 1, p * part_rows : (p + 1) * part_rows] = relay[way, p]

    def radial_arrived():
        @pl.when(has_in)
        def _():
            for c in outward:
                c.wait_recv()

        @pl.when(has_out)
        def _():
            for c in inward:
                c.wait_recv()

        @pl.when(at_inner)
        def _():
            st[:, 0] = st[:, 1]

        @pl.when(at_outer)
        def _():
            st[:, rows + 1] = st[:, rows]

    def radial_sent():
        @pl.when(has_out)
        def _():
            for c in outward:
                c.wait_send()

        @pl.when(has_in)
        def _():
            for c in inward:
                c.wait_send()

        for way in range(2):
            for p in range(half):
                carries, hands_on, onward, first = seam_part(way, p)

                @pl.when(hands_on)
                def _():
                    onward.wait_send()

    for c in loads[1]:
        c.wait()
    lax.fori_loop(1, tiles, packing, 0)
    for c in azimuthal[1]:
        c.start()
    get_shifts.wait()

    total = groups * rows

    def radius(index):
        return 1.0 + 2.0 * (index.astype(jnp.float32) + 0.5) / total

    def upwind(face, low, high):
        return face * jnp.where(face > 0, low, high)

    def compute(row, t):
        t0 = pl.multiple_of(t * SUB, SUB)
        at = pl.ds(t0, SUB)
        at_dn = pl.ds(pl.multiple_of(jnp.maximum(t - 1, 0) * SUB, SUB), SUB)
        at_up = pl.ds(pl.multiple_of(jnp.minimum(t + 1, tiles - 1) * SUB, SUB), SUB)
        index = pos * rows + row
        here = radius(index)
        face_up = 0.5 * (here + radius(index + 1))
        face_dn = 0.5 * (radius(index - 1) + here)
        area = jnp.full((SUB, LANES), here * here, jnp.float32)
        w_up = jnp.full((SUB, LANES), face_up * face_up, jnp.float32) / area
        w_dn = jnp.full((SUB, LANES), face_dn * face_dn, jnp.float32) / area
        w_up = jnp.where(index == total - 1, 0.0, w_up)
        w_dn = jnp.where(index == 0, 0.0, w_dn)
        before = halo[0, t]
        after = halo[1, t]
        q = [[st[f, row + 1, at, h * LANES : (h + 1) * LANES] for h in range(2)] for f in range(FIELDS)]
        back, ahead = [], []
        for f in range(FIELDS):
            k = f * rows + row
            b = pltpu.roll(before, (LANES - k) % LANES, 1)
            a = pltpu.roll(after, LANES - 1 - k, 1)
            low, high = q[f]
            low_r, high_r = pltpu.roll(low, 1, 1), pltpu.roll(high, 1, 1)
            low_l, high_l = pltpu.roll(low, LANES - 1, 1), pltpu.roll(high, LANES - 1, 1)
            back.append([jnp.where(lane == 0, b, low_r), jnp.where(lane == 0, low_r, high_r)])
            ahead.append(
                [jnp.where(lane == LANES - 1, high_l, low_l), jnp.where(lane == LANES - 1, a, high_l)]
            )
        for h in range(2):
            cols = slice(h * LANES, (h + 1) * LANES)
            c = [q[f][h] for f in range(FIELDS)]
            inner = [st[f, row, at, cols] for f in range(FIELDS)]
            outer = [st[f, row + 2, at, cols] for f in range(FIELDS)]
            above, below = [], []
            for f in range(FIELDS):
                prev = st[f, row + 1, at_dn, cols]
                nxt = st[f, row + 1, at_up, cols]
                below.append(pltpu.roll(jnp.where(sub == SUB - 1, prev, c[f]), 1, 0))
                above.append(pltpu.roll(jnp.where(sub == 0, nxt, c[f]), SUB - 1, 0))
            below[4] = jnp.where(t0 + sub == 0, c[4], below[4])
            above[4] = jnp.where(t0 + sub == tiles * SUB - 1, c[4], above[4])
            inv = 1.0 / c[0]
            v_r, v_p, v_t = c[1] * inv, c[2] * inv, c[3] * inv
            r_up = 0.5 * (v_r + outer[1] / outer[0])
            r_dn = 0.5 * (v_r + inner[1] / inner[0])
            p_up = 0.5 * (v_p + ahead[2][h] / ahead[0][h])
            p_dn = 0.5 * (v_p + back[2][h] / back[0][h])
            t_up_v = jnp.where(t0 + sub == tiles * SUB - 1, 0.0, 0.5 * (v_t + above[3] / above[0]))
            t_dn_v = jnp.where(t0 + sub == 0, 0.0, 0.5 * (v_t + below[3] / below[0]))
            r_up_w, r_dn_w = r_up * w_up, r_dn * w_dn
            for f in range(FIELDS):
                out = c[f]
                out -= r_up_w * jnp.where(r_up > 0, c[f], outer[f]) - r_dn_w * jnp.where(r_dn > 0, inner[f], c[f])
                out -= upwind(t_up_v, c[f], above[f]) - upwind(t_dn_v, below[f], c[f])
                out -= upwind(p_up, c[f], ahead[f][h]) - upwind(p_dn, back[f][h], c[f])
                if f == 1:
                    out -= 0.5 * (0.5 * (0.4 * outer[4] - 0.4 * inner[4]))
                if f == 2:
                    out -= 0.5 * (0.5 * (0.4 * ahead[4][h] - 0.4 * back[4][h]))
                if f == 3:
                    out -= 0.5 * (0.5 * (0.4 * above[4] - 0.4 * below[4]))
                send[row, t, h, f] = out

    def whole_row(row, c):
        lax.fori_loop(0, per, lambda p, _: (compute(row, c * per + p), 0)[1], 0)

    def turn_of(c):
        return (c % 2 * 4 + c // 2 % 2 * 2 + c // 4) * (rows // 8) % rows

    def first_leg(c, row):
        part = send.at[row, pl.ds(c * per, per)]
        return part, whole[c].at[me]

    def produce(c, wanted):
        def step(k, _):
            to = peer(me, k)
            row = (to + n - turn_of(c)) % n

            def do():
                whole_row(row, c)
                part, place = first_leg(c, row)

                @pl.when(to != me)
                def _():
                    remote(part, place, s1.at[c], r1.at[c], az=to).start()

                @pl.when(to == me)
                def _():
                    pltpu.make_async_copy(part, place, own1.at[c]).start()

            edge = (row == 0) | (row == rows - 1)
            if wanted == "every":
                do()
            elif wanted == "edges":
                pl.when(edge)(do)
            else:
                pl.when(jnp.logical_not(edge))(do)
            return 0

        lax.fori_loop(1, n + 1, step, 0)

    for c in azimuthal[0]:
        c.wait()
    for c in range(chunks):
        produce(c, "inside" if c < early else "every")
        if c == 0:
            for a in azimuthal[1]:
                a.wait()
        if 1 <= c - early + half + 1 <= half:
            seam(c - early + half + 1)
        if c == early - 1:
            radial_arrived()
            seam_into_state()
            for e in range(early):
                produce(e, "edges")

    def second_leg(c, b):
        thetas = pl.ds(c * per * SUB, per * SUB)
        return turned.at[b, :, thetas], landed.at[(me + n - turn_of(c)) % n, :, thetas]

    for c in range(chunks):
        wait_bytes(whole[c].at[pl.ds(0, n - 1)], r1.at[c])
        pltpu.make_async_copy(send.at[me, pl.ds(c * per, per)], whole[c].at[me], own1.at[c]).wait()

        amount = amounts[(me + n - turn_of(c)) % n]
        skip = amount // LANES
        turn = amount % LANES

        def give(k, _, c=c, skip=skip, turn=turn):
            b = peer(me, k)
            for h in range(2):
                a = (2 * b + h - skip) & (2 * n - 1)
                z = (2 * b + h - skip - 1) & (2 * n - 1)
                for p in range(per):
                    for f in range(FIELDS):
                        late = pltpu.roll(whole[c][a // 2, p, a % 2, f], turn, 1)
                        soon = pltpu.roll(whole[c][z // 2, p, z % 2, f], turn, 1)
                        value = jnp.where(lane >= turn, late, soon)
                        turned[b, f, pl.ds((c * per + p) * SUB, SUB), h * LANES : (h + 1) * LANES] = value

            src, dst = second_leg(c, b)

            @pl.when(b != me)
            def _():
                remote(src, dst, s2, r2, az=b).start()

            @pl.when(b == me)
            def _():
                pltpu.make_async_copy(src, dst, own2).start()

            return 0

        lax.fori_loop(1, n + 1, give, 0)

    for c in range(chunks):
        wait_bytes(send.at[pl.ds(0, n - 1), pl.ds(c * per, per)], s1.at[c])
    wait_bytes(landed.at[pl.ds(0, n - 1)], s2)
    wait_bytes(landed.at[me], own2)
    wait_bytes(landed.at[pl.ds(0, n - 1)], r2)

    radial_sent()


def deliver(landed, den_o, mom_o, en_o, sems):
    rows = den_o.shape[0]
    parts = sems.shape[0]
    copies = []
    for p in range(parts):
        at = pl.ds(p * (rows // parts), rows // parts)
        copies.append(pltpu.make_async_copy(landed.at[at, 0], den_o.at[at], sems.at[p, 0]))
        for f in range(3):
            copies.append(pltpu.make_async_copy(landed.at[at, 1 + f], mom_o.at[f, at], sems.at[p, 1 + f]))
        copies.append(pltpu.make_async_copy(landed.at[at, 4], en_o.at[at], sems.at[p, 4]))
    for c in copies:
        c.start()
    for c in copies:
        c.wait()


def per_device(density, momenta, energy, shifts):
    rows, thetas, width = density.shape
    n = lax.axis_size("az")
    tiles = thetas // SUB
    chunks, early = 8, 6
    per = tiles // chunks
    half = lax.axis_size("rad") // 2
    dma = pltpu.SemaphoreType.DMA
    f32 = jnp.float32
    hbm = pl.BlockSpec(memory_space=pltpu.HBM)
    landed = pl.pallas_call(
        functools.partial(kernel, chunks, early),
        out_shape=pltpu.VMEM((n, FIELDS, thetas, width), f32),
        in_specs=[hbm] * 4,
        out_specs=pl.BlockSpec(memory_space=pltpu.VMEM),
        scratch_shapes=[
            pltpu.SMEM((rows,), jnp.int32),
            pltpu.VMEM((FIELDS, rows + 2, thetas, width), f32),
            pltpu.VMEM((rows, tiles, 2, FIELDS, SUB, LANES), f32),
            pltpu.VMEM((n, FIELDS, thetas, width), f32),
            pltpu.VMEM((2, tiles, SUB, LANES), f32),
            pltpu.VMEM((2, tiles, SUB, LANES), f32),
            pltpu.VMEM((2, half, FIELDS, thetas // half, width), f32),
            *[pltpu.VMEM((n, per, 2, FIELDS, SUB, LANES), f32) for _ in range(chunks)],
            dma((2, 3)),
            dma,
            dma((2, 3)),
            dma((2, 3)),
            dma((2, half)),
            dma((2, half)),
            dma((2, 2)),
            dma((2, 2)),
            dma((chunks,)),
            dma((chunks,)),
            dma((chunks,)),
            dma,
            dma,
            dma,
        ],
        compiler_params=pltpu.CompilerParams(
            collective_id=0, has_side_effects=True, vmem_limit_bytes=56 * 2**20
        ),
        name="transport",
    )(density, momenta, energy, shifts)
    return pl.pallas_call(
        deliver,
        out_shape=[jax.ShapeDtypeStruct(x.shape, f32) for x in (density, momenta, energy)],
        in_specs=[pl.BlockSpec(memory_space=pl.ANY)],
        out_specs=[pl.BlockSpec(memory_space=pl.ANY)] * 3,
        scratch_shapes=[dma((1, FIELDS))],
        compiler_params=pltpu.CompilerParams(vmem_limit_bytes=2**20),
        name="deliver",
    )(landed)


def solution(mesh):
    return jax.shard_map(
        per_device,
        mesh=mesh,
        in_specs=(P("rad", None, "az"), P(None, "rad", None, "az"), P("rad", None, "az"), P("rad")),
        out_specs=(P("rad", None, "az"), P(None, "rad", None, "az"), P("rad", None, "az")),
        check_vma=False,
    )
```

```python
import functools

import jax
import jax.numpy as jnp
from jax import lax
from jax.experimental import pallas as pl
from jax.experimental.pallas import tpu as pltpu
from jax.sharding import PartitionSpec as P

MESH = pl.DeviceIdType.MESH
LANES = 128
SUB = 8
FIELDS = 5


def remote(src, dst, send, recv, **where):
    return pltpu.make_async_remote_copy(
        src_ref=src, dst_ref=dst, send_sem=send, recv_sem=recv, device_id=where, device_id_type=MESH
    )


def wait_bytes(ref, sem):
    pltpu.make_async_copy(ref, ref, sem).wait()


def peer(me, k):
    y = (me // 4 + k) % 4
    x = (me // 2 + k // 4) % 2
    core = (me + k // 8) % 2
    return y * 4 + x * 2 + core


def kernel(chunks, early, den, mom, en, shifts, landed, *refs):
    amounts, st, send, turned, pack, halo, relay = refs[:7]
    whole = refs[7 : 7 + chunks]
    in_sem, shift_sem, rad_send, rad_recv, relay_send, relay_recv, az_send, az_recv, s1, r1, own1, s2, r2, own2 = refs[7 + chunks :]
    rows = den.shape[0]
    tiles = den.shape[1] // SUB
    per = tiles // chunks
    me = lax.axis_index("az")
    n = lax.axis_size("az")
    pos = lax.axis_index("rad")
    groups = lax.axis_size("rad")
    at_inner = pos == 0
    at_outer = pos == groups - 1

    def load(j, first, count):
        at = pl.ds(first * SUB, count * SUB)
        return [
            pltpu.make_async_copy(den.at[:, at], st.at[0, pl.ds(1, rows), at], in_sem.at[j, 0]),
            pltpu.make_async_copy(mom.at[:, :, at], st.at[pl.ds(1, 3), pl.ds(1, rows), at], in_sem.at[j, 1]),
            pltpu.make_async_copy(en.at[:, at], st.at[4, pl.ds(1, rows), at], in_sem.at[j, 2]),
        ]

    loads = [load(0, 0, 2), load(1, 2, tiles - 2)]
    get_shifts = pltpu.make_async_copy(shifts, amounts, shift_sem)
    for part in loads:
        for c in part:
            c.start()
    get_shifts.start()

    barrier = pltpu.get_barrier_semaphore()

    def greet(k, _):
        pl.semaphore_signal(barrier, 1, device_id={"az": peer(me, k)}, device_id_type=MESH)
        return 0

    lax.fori_loop(1, n, greet, 0)

    half = groups // 2
    across = (pos + half) % groups
    has_out = jnp.logical_not(at_outer) & (pos != half - 1)
    has_in = jnp.logical_not(at_inner) & (pos != half)
    pl.semaphore_signal(barrier, 1, device_id={"rad": across}, device_id_type=MESH)

    @pl.when(has_out)
    def _():
        pl.semaphore_signal(barrier, 1, device_id={"rad": pos + 1}, device_id_type=MESH)

    @pl.when(has_in)
    def _():
        pl.semaphore_signal(barrier, 1, device_id={"rad": pos - 1}, device_id_type=MESH)

    lane = lax.broadcasted_iota(jnp.int32, (SUB, LANES), 1)
    sub = lax.broadcasted_iota(jnp.int32, (SUB, LANES), 0)

    def packing(t, _):
        at = pl.ds(pl.multiple_of(t * SUB, SUB), SUB)
        first = jnp.zeros((SUB, LANES), jnp.float32)
        last = jnp.zeros((SUB, LANES), jnp.float32)
        for f in range(FIELDS):
            for i in range(rows):
                k = f * rows + i
                low = st[f, 1 + i, at, 0:LANES]
                high = st[f, 1 + i, at, LANES : 2 * LANES]
                first = jnp.where(lane == k, pltpu.roll(low, k, 1) if k else low, first)
                last = jnp.where(lane == k, pltpu.roll(high, k + 1, 1), last)
        pack[0, t] = first
        pack[1, t] = last
        return 0

    def edges(j, first, count):
        at = pl.ds(first, count)
        return [
            remote(pack.at[1, at], halo.at[0, at], az_send.at[j, 0], az_recv.at[j, 0], az=(me + 1) % n),
            remote(pack.at[0, at], halo.at[1, at], az_send.at[j, 1], az_recv.at[j, 1], az=(me + n - 1) % n),
        ]

    azimuthal = [edges(0, 0, 1), edges(1, 1, tiles - 1)]
    for c in loads[0]:
        c.wait()
    packing(0, 0)
    pl.semaphore_wait(barrier, n + jnp.where(has_out, 1, 0) + jnp.where(has_in, 1, 0))
    for c in azimuthal[0]:
        c.start()

    def radial(way, row, slot, to):
        srcs = [den.at[row], mom.at[:, row], en.at[row]]
        dsts = [st.at[0, slot], st.at[pl.ds(1, 3), slot], st.at[4, slot]]
        return [remote(a, b, rad_send.at[way, j], rad_recv.at[way, j], rad=to) for j, (a, b) in enumerate(zip(srcs, dsts))]

    outward = radial(0, rows - 1, 0, (pos + 1) % groups)
    inward = radial(1, 0, rows + 1, (pos + groups - 1) % groups)

    part_rows = tiles * SUB // half
    low = pos < half
    place = pos % half

    def seam_part(way, p):
        carries = jnp.where(low, p <= place, p >= place)
        crossing = low if way == 0 else jnp.logical_not(low)
        step = groups - 1 if way == 0 else 1
        to = jnp.where(crossing & (p == place), across, (pos + step) % groups)
        last = pos == (half if way == 0 else half - 1)
        at = pl.ds(p * part_rows, part_rows)
        row = rows - 1 if way == 0 else 0
        edge = [den.at[row, at], mom.at[:, row, at], en.at[row, at]]
        slot = [relay.at[way, p, 0], relay.at[way, p, pl.ds(1, 3)], relay.at[way, p, 4]]

        def copy(src, dst):
            return remote(src, dst, relay_send.at[way, p], relay_recv.at[way, p], rad=to)

        first = [copy(a, b) for a, b in zip(edge, slot)]
        return carries, carries & jnp.logical_not(last), copy(relay.at[way, p], relay.at[way, p]), first

    def seam(stage):
        for way in range(2):
            hops = jnp.where(low, half - 1 - place, half - place) if way == 0 else jnp.where(low, place + 1, place)

            @pl.when(hops == stage)
            def _():
                for p in range(half):
                    carries, hands_on, onward, first = seam_part(way, p)
                    if stage == 0:
                        @pl.when(carries)
                        def _():
                            for a in first:
                                a.start()
                    else:
                        @pl.when(carries)
                        def _():
                            onward.wait_recv()

                        @pl.when(hands_on)
                        def _():
                            onward.start()

    seam(0)

    def radial_start():
        @pl.when(has_out)
        def _():
            for c in outward:
                c.start()

        @pl.when(has_in)
        def _():
            for c in inward:
                c.start()

    def seam_into_state():
        for way in range(2):
            @pl.when(pos == (half if way == 0 else half - 1))
            def _():
                for p in range(half):
                    st[:, 0 if way == 0 else rows + 1, p * part_rows : (p + 1) * part_rows] = relay[way, p]

    def radial_arrived():
        @pl.when(has_in)
        def _():
            for c in outward:
                c.wait_recv()

        @pl.when(has_out)
        def _():
            for c in inward:
                c.wait_recv()

        @pl.when(at_inner)
        def _():
            st[:, 0] = st[:, 1]

        @pl.when(at_outer)
        def _():
            st[:, rows + 1] = st[:, rows]

    def radial_sent():
        @pl.when(has_out)
        def _():
            for c in outward:
                c.wait_send()

        @pl.when(has_in)
        def _():
            for c in inward:
                c.wait_send()

        for way in range(2):
            for p in range(half):
                carries, hands_on, onward, first = seam_part(way, p)

                @pl.when(hands_on)
                def _():
                    onward.wait_send()

    for c in loads[1]:
        c.wait()
    lax.fori_loop(1, tiles, packing, 0)
    for c in azimuthal[1]:
        c.start()
    get_shifts.wait()

    total = groups * rows

    def radius(index):
        return 1.0 + 2.0 * (index.astype(jnp.float32) + 0.5) / total

    def upwind(face, low, high):
        return face * jnp.where(face > 0, low, high)

    def compute(row, t):
        t0 = pl.multiple_of(t * SUB, SUB)
        at = pl.ds(t0, SUB)
        at_dn = pl.ds(pl.multiple_of(jnp.maximum(t - 1, 0) * SUB, SUB), SUB)
        at_up = pl.ds(pl.multiple_of(jnp.minimum(t + 1, tiles - 1) * SUB, SUB), SUB)
        index = pos * rows + row
        here = radius(index)
        face_up = 0.5 * (here + radius(index + 1))
        face_dn = 0.5 * (radius(index - 1) + here)
        area = jnp.full((SUB, LANES), here * here, jnp.float32)
        w_up = jnp.full((SUB, LANES), face_up * face_up, jnp.float32) / area
        w_dn = jnp.full((SUB, LANES), face_dn * face_dn, jnp.float32) / area
        w_up = jnp.where(index == total - 1, 0.0, w_up)
        w_dn = jnp.where(index == 0, 0.0, w_dn)
        before = halo[0, t]
        after = halo[1, t]
        q = [[st[f, row + 1, at, h * LANES : (h + 1) * LANES] for h in range(2)] for f in range(FIELDS)]
        back, ahead = [], []
        for f in range(FIELDS):
            k = f * rows + row
            b = pltpu.roll(before, (LANES - k) % LANES, 1)
            a = pltpu.roll(after, LANES - 1 - k, 1)
            low, high = q[f]
            low_r, high_r = pltpu.roll(low, 1, 1), pltpu.roll(high, 1, 1)
            low_l, high_l = pltpu.roll(low, LANES - 1, 1), pltpu.roll(high, LANES - 1, 1)
            back.append([jnp.where(lane == 0, b, low_r), jnp.where(lane == 0, low_r, high_r)])
            ahead.append(
                [jnp.where(lane == LANES - 1, high_l, low_l), jnp.where(lane == LANES - 1, a, high_l)]
            )
        for h in range(2):
            cols = slice(h * LANES, (h + 1) * LANES)
            c = [q[f][h] for f in range(FIELDS)]
            inner = [st[f, row, at, cols] for f in range(FIELDS)]
            outer = [st[f, row + 2, at, cols] for f in range(FIELDS)]
            above, below = [], []
            for f in range(FIELDS):
                prev = st[f, row + 1, at_dn, cols]
                nxt = st[f, row + 1, at_up, cols]
                below.append(pltpu.roll(jnp.where(sub == SUB - 1, prev, c[f]), 1, 0))
                above.append(pltpu.roll(jnp.where(sub == 0, nxt, c[f]), SUB - 1, 0))
            below[4] = jnp.where(t0 + sub == 0, c[4], below[4])
            above[4] = jnp.where(t0 + sub == tiles * SUB - 1, c[4], above[4])
            inv = 1.0 / c[0]
            v_r, v_p, v_t = c[1] * inv, c[2] * inv, c[3] * inv
            r_up = 0.5 * (v_r + outer[1] / outer[0])
            r_dn = 0.5 * (v_r + inner[1] / inner[0])
            p_up = 0.5 * (v_p + ahead[2][h] / ahead[0][h])
            p_dn = 0.5 * (v_p + back[2][h] / back[0][h])
            t_up_v = jnp.where(t0 + sub == tiles * SUB - 1, 0.0, 0.5 * (v_t + above[3] / above[0]))
            t_dn_v = jnp.where(t0 + sub == 0, 0.0, 0.5 * (v_t + below[3] / below[0]))
            r_up_w, r_dn_w = r_up * w_up, r_dn * w_dn
            for f in range(FIELDS):
                out = c[f]
                out -= r_up_w * jnp.where(r_up > 0, c[f], outer[f]) - r_dn_w * jnp.where(r_dn > 0, inner[f], c[f])
                out -= upwind(t_up_v, c[f], above[f]) - upwind(t_dn_v, below[f], c[f])
                out -= upwind(p_up, c[f], ahead[f][h]) - upwind(p_dn, back[f][h], c[f])
                if f == 1:
                    out -= 0.5 * (0.5 * (0.4 * outer[4] - 0.4 * inner[4]))
                if f == 2:
                    out -= 0.5 * (0.5 * (0.4 * ahead[4][h] - 0.4 * back[4][h]))
                if f == 3:
                    out -= 0.5 * (0.5 * (0.4 * above[4] - 0.4 * below[4]))
                send[row, t, h, f] = out

    def whole_row(row, c):
        lax.fori_loop(0, per, lambda p, _: (compute(row, c * per + p), 0)[1], 0)

    def turn_of(c):
        return (c % 2 * 4 + c // 2 % 2 * 2 + c // 4) * (rows // 8) % rows

    def first_leg(c, row):
        part = send.at[row, pl.ds(c * per, per)]
        return part, whole[c].at[me]

    def produce(c, wanted):
        def step(k, _):
            to = peer(me, k)
            row = (to + n - turn_of(c)) % n

            def do():
                whole_row(row, c)
                part, place = first_leg(c, row)

                @pl.when(to != me)
                def _():
                    remote(part, place, s1.at[c], r1.at[c], az=to).start()

                @pl.when(to == me)
                def _():
                    pltpu.make_async_copy(part, place, own1.at[c]).start()

            edge = (row == 0) | (row == rows - 1)
            if wanted == "every":
                do()
            elif wanted == "edges":
                pl.when(edge)(do)
            else:
                pl.when(jnp.logical_not(edge))(do)
            return 0

        lax.fori_loop(0, rows, step, 0)

    for c in azimuthal[0]:
        c.wait()
    for c in range(chunks):
        produce(c, "inside" if c < early else "every")
        if c == 0:
            radial_start()
            for a in azimuthal[1]:
                a.wait()
        if 1 <= c - early + half + 1 <= half:
            seam(c - early + half + 1)
        if c == early - 1:
            radial_arrived()
            seam_into_state()
            for e in range(early):
                produce(e, "edges")

    def second_leg(c, b):
        thetas = pl.ds(c * per * SUB, per * SUB)
        return turned.at[b, :, thetas], landed.at[(me + n - turn_of(c)) % n, :, thetas]

    for c in range(chunks):
        wait_bytes(whole[c].at[pl.ds(0, n - 1)], r1.at[c])
        pltpu.make_async_copy(send.at[me, pl.ds(c * per, per)], whole[c].at[me], own1.at[c]).wait()

        amount = amounts[(me + n - turn_of(c)) % n]
        skip = amount // LANES
        turn = amount % LANES

        def give(k, _, c=c, skip=skip, turn=turn):
            b = peer(me, k)
            for h in range(2):
                a = (2 * b + h - skip) & (2 * n - 1)
                z = (2 * b + h - skip - 1) & (2 * n - 1)
                for p in range(per):
                    for f in range(FIELDS):
                        late = pltpu.roll(whole[c][a // 2, p, a % 2, f], turn, 1)
                        soon = pltpu.roll(whole[c][z // 2, p, z % 2, f], turn, 1)
                        value = jnp.where(lane >= turn, late, soon)
                        turned[b, f, pl.ds((c * per + p) * SUB, SUB), h * LANES : (h + 1) * LANES] = value

            src, dst = second_leg(c, b)

            @pl.when(b != me)
            def _():
                remote(src, dst, s2, r2, az=b).start()

            @pl.when(b == me)
            def _():
                pltpu.make_async_copy(src, dst, own2).start()

            return 0

        lax.fori_loop(0, n, give, 0)

    for c in range(chunks):
        wait_bytes(send.at[pl.ds(0, n - 1), pl.ds(c * per, per)], s1.at[c])
    wait_bytes(landed.at[pl.ds(0, n - 1)], s2)
    wait_bytes(landed.at[me], own2)
    wait_bytes(landed.at[pl.ds(0, n - 1)], r2)

    radial_sent()


def deliver(landed, den_o, mom_o, en_o, sems):
    rows = den_o.shape[0]
    parts = sems.shape[0]
    copies = []
    for p in range(parts):
        at = pl.ds(p * (rows // parts), rows // parts)
        copies.append(pltpu.make_async_copy(landed.at[at, 0], den_o.at[at], sems.at[p, 0]))
        for f in range(3):
            copies.append(pltpu.make_async_copy(landed.at[at, 1 + f], mom_o.at[f, at], sems.at[p, 1 + f]))
        copies.append(pltpu.make_async_copy(landed.at[at, 4], en_o.at[at], sems.at[p, 4]))
    for c in copies:
        c.start()
    for c in copies:
        c.wait()


def per_device(density, momenta, energy, shifts):
    rows, thetas, width = density.shape
    n = lax.axis_size("az")
    tiles = thetas // SUB
    chunks, early = 8, 6
    per = tiles // chunks
    half = lax.axis_size("rad") // 2
    dma = pltpu.SemaphoreType.DMA
    f32 = jnp.float32
    hbm = pl.BlockSpec(memory_space=pltpu.HBM)
    landed = pl.pallas_call(
        functools.partial(kernel, chunks, early),
        out_shape=pltpu.VMEM((n, FIELDS, thetas, width), f32),
        in_specs=[hbm] * 4,
        out_specs=pl.BlockSpec(memory_space=pltpu.VMEM),
        scratch_shapes=[
            pltpu.SMEM((rows,), jnp.int32),
            pltpu.VMEM((FIELDS, rows + 2, thetas, width), f32),
            pltpu.VMEM((rows, tiles, 2, FIELDS, SUB, LANES), f32),
            pltpu.VMEM((n, FIELDS, thetas, width), f32),
            pltpu.VMEM((2, tiles, SUB, LANES), f32),
            pltpu.VMEM((2, tiles, SUB, LANES), f32),
            pltpu.VMEM((2, half, FIELDS, thetas // half, width), f32),
            *[pltpu.VMEM((n, per, 2, FIELDS, SUB, LANES), f32) for _ in range(chunks)],
            dma((2, 3)),
            dma,
            dma((2, 3)),
            dma((2, 3)),
            dma((2, half)),
            dma((2, half)),
            dma((2, 2)),
            dma((2, 2)),
            dma((chunks,)),
            dma((chunks,)),
            dma((chunks,)),
            dma,
            dma,
            dma,
        ],
        compiler_params=pltpu.CompilerParams(
            collective_id=0, has_side_effects=True, vmem_limit_bytes=56 * 2**20
        ),
        name="transport",
    )(density, momenta, energy, shifts)
    return pl.pallas_call(
        deliver,
        out_shape=[jax.ShapeDtypeStruct(x.shape, f32) for x in (density, momenta, energy)],
        in_specs=[pl.BlockSpec(memory_space=pl.ANY)],
        out_specs=[pl.BlockSpec(memory_space=pl.ANY)] * 3,
        scratch_shapes=[dma((4, FIELDS))],
        compiler_params=pltpu.CompilerParams(vmem_limit_bytes=2**20),
        name="deliver",
    )(landed)


def solution(mesh):
    return jax.shard_map(
        per_device,
        mesh=mesh,
        in_specs=(P("rad", None, "az"), P(None, "rad", None, "az"), P("rad", None, "az"), P("rad")),
        out_specs=(P("rad", None, "az"), P(None, "rad", None, "az"), P("rad", None, "az")),
        check_vma=False,
    )
```
